128 devices in a mesh: outer: 8 (over y, core), inner: 16 (over z, x).
Axes of the slice: x: 4, y: 4, z: 4, core: 2. Of those that a mesh axis runs over, the one named last changes fastest.
Arguments:
- byte_states: bfloat16 [65536, 1024], P(('outer', 'inner')), may hold values from -6 to 6
- patch_vectors: bfloat16 [16384, 1024], P(('outer', 'inner')), may hold values from -6 to 6
- patch_starts: int32 [16384], P(('outer', 'inner')), may hold values from 0 to 65535, as said below
- beta_codes: int32 [65536, 8], P(('outer', 'inner')), may hold values from 0 to 8, as said below
- w_qkv: bfloat16 [1024, 3072], replicated, may hold values from -0.1875 to 0.1875
- conv_taps: float32 [4, 3072], replicated, may hold values from -3 to 3
- norm_gain: float32 [1024], replicated, may hold values from 0.5 to 1.5
- w_out: bfloat16 [1024, 1024], replicated, may hold values from -0.1875 to 0.1875
Outputs:
- mixed_bytes: bfloat16 [65536, 1024], P(('outer', 'inner'))
The draws below stay inside these ranges and needn't reach their ends.
Inputs may be any that keep to these rules, and one draw needn't show every extreme that they name: `patch_starts`: strictly increasing; entries j * 128 to (j + 1) * 128 - 1 lie in [j * 512, (j + 1) * 512); the first entry is 0. `beta_codes`: code c stands for beta = c / 4.
All inputs are finite; a program needn't handle non-finite values.
Results may differ from the reference program's by a relative error of at most 0.012.
The reference program's roundings to bfloat16 on the way (of `hidden`, `projected` and `normed`) count: a program that leaves them out, or rounds other values in their place, can miss the bound.
Values may be sent and summed in bfloat16 or wider, within the bound.
A program may use at most 320 MiB of HBM per device.

```python
import jax
import jax.numpy as jnp
from jax import lax

HEADS = 8
HEAD = 128
D = 1024
TOK_DEV = 512
SEQUENCE_TOKENS = 65536
PATCH_DEV = 128
PATCHES = 16384


def draw_patch_starts(key, part):
    device_count = SEQUENCE_TOKENS // TOK_DEV

    def draw_block(subkey):
        order = jax.random.permutation(subkey, TOK_DEV)
        return jnp.sort(order[:PATCH_DEV])
    block_keys = jax.random.split(key, device_count)
    chosen = jax.vmap(draw_block)(block_keys).astype(jnp.int32)
    offset_rows = jnp.arange(device_count, dtype=jnp.int32)[:, None] * TOK_DEV
    starts_all = chosen + offset_rows
    starts_all = starts_all.at[0, 0].set(0).at[device_count - 1, PATCH_DEV - 1].set(SEQUENCE_TOKENS - 1)
    return starts_all.reshape(-1)


def draw_beta_codes(key, part):
    key_write_rate, key_enabled_flag, key_intensity_level, key_surge_flag = jax.random.split(key, 4)
    top_exponent = (SEQUENCE_TOKENS // HEAD).bit_length()
    rate_bits = jax.random.randint(key_write_rate, (1, HEADS), 0, top_exponent + 1)
    dice_rolls = jax.random.randint(key_enabled_flag, (SEQUENCE_TOKENS, HEADS), 0, 2 ** top_exponent)
    active = dice_rolls & jnp.left_shift(1, rate_bits) - 1 == 0
    levels = jax.random.randint(key_intensity_level, (SEQUENCE_TOKENS, HEADS), 1, 9)
    codes_all = jnp.where(active, levels, 0)
    surge_start_points = jax.random.randint(key_surge_flag, (4,), 0, SEQUENCE_TOKENS)
    token_positions = jnp.arange(SEQUENCE_TOKENS, dtype=jnp.int32)[:, None]
    position_distance = token_positions - surge_start_points[None, :]
    inside = jnp.any((position_distance >= 0) & (position_distance < HEAD // 4), axis=1)
    codes_all = jnp.where(inside[:, None], 4, codes_all)
    codes_all = codes_all.at[0, 0].set(8).at[1, 0].set(0)
    return codes_all.astype(jnp.int32)


def block_scale(key, shape, cuts, low, largest):
    level, own = 1.0, jax.random.fold_in(key, 6)
    for axis_at, parts in cuts:
        heights = jnp.exp(jax.random.uniform(jax.random.fold_in(own, axis_at), (parts,), jnp.float32, low / len(cuts), largest / len(cuts)))
        level = level * jnp.repeat(heights, shape[axis_at] // parts).reshape([-1 if axis == axis_at else 1 for axis in range(len(shape))])
    return level


def scatter_about(rng, dims, deviation, reach, shards=(), kind=jnp.bfloat16):
    gain = block_scale(rng, dims, shards, -0.22, 0.18) if shards else 1.0
    drawn = jax.random.normal(rng, dims, jnp.float32) * deviation * gain
    return jnp.minimum(jnp.maximum(drawn, -reach), reach).astype(kind)


def setup_inputs(seed: int = 0) -> dict:
    keys = jax.random.split(jax.random.key(seed), 9)
    return {
        "byte_states": scatter_about(keys[0], (SEQUENCE_TOKENS, D), 1.0, 6.0, ((0, 128),)),
        "patch_vectors": scatter_about(keys[1], (PATCHES, D), 1.0, 6.0, ((0, 128),)),
        "patch_starts": draw_patch_starts(jax.random.fold_in(keys[8], 71), 0),
        "beta_codes": draw_beta_codes(jax.random.fold_in(keys[8], 71), 0),
        "w_qkv": scatter_about(keys[4], (D, 3 * D), D ** -0.5, 0.1875),
        "conv_taps": scatter_about(keys[5], (4, 3 * D), 0.6, 3.0, (), jnp.float32),
        "norm_gain": jnp.clip(jax.random.uniform(keys[6], (D,), jnp.float32, 0.5, 1.5), 0.5, 1.5),
        "w_out": scatter_about(keys[7], (D, D), D ** -0.5, 0.1875),
    }


exact_arithmetic_mode = lax.Precision.HIGHEST
norm_eps = 1e-06

def causal_conv(extended, conv_taps, row_count):
    running = jnp.zeros((row_count, extended.shape[1]), jnp.float32)
    for offset in range(4):
        running = running + conv_taps[offset][None, :] * extended[offset:offset + row_count]
    return running

def reference(byte_states, patch_vectors, patch_starts, beta_codes, w_qkv, conv_taps, norm_gain, w_out):
    token_positions = jnp.arange(SEQUENCE_TOKENS, dtype=jnp.int32)
    patch_index = (jnp.searchsorted(patch_starts, token_positions, side='right') - 1).astype(jnp.int32)
    block_count = SEQUENCE_TOKENS // TOK_DEV
    states_blocks = byte_states.reshape(block_count, TOK_DEV, D)
    index_blocks = patch_index.reshape(block_count, TOK_DEV)
    code_blocks = beta_codes.reshape(block_count, TOK_DEV, HEADS)
    gain_heads = norm_gain.reshape(HEADS, HEAD)

    def token_step(current_state, inputs):
        single_query_row, single_key_row, value_row, beta_row = inputs
        predicted_values = jnp.einsum('du,duz->dz', single_key_row, current_state, precision=exact_arithmetic_mode)
        current_state = current_state + beta_row[:, None, None] * single_key_row[:, :, None] * (value_row - predicted_values)[:, None, :]
        single_output_row = jnp.einsum('du,duz->dz', single_query_row, current_state, precision=exact_arithmetic_mode)
        return (current_state, single_output_row)

    def block_step(carry, inputs):
        current_state, rim_rows = carry
        block_states, block_index, block_codes = inputs
        fetched = jnp.take(patch_vectors, block_index, axis=0)
        hidden = (block_states.astype(jnp.float32) + fetched.astype(jnp.float32)).astype(jnp.bfloat16)
        projected = jnp.dot(hidden, w_qkv, preferred_element_type=jnp.float32).astype(jnp.bfloat16)
        extended = jnp.concatenate([rim_rows, projected], axis=0).astype(jnp.float32)
        activated = jax.nn.silu(causal_conv(extended, conv_taps, TOK_DEV))
        queries = activated[:, :D].reshape(TOK_DEV, HEADS, HEAD)
        raw_keys = activated[:, D:2 * D].reshape(TOK_DEV, HEADS, HEAD)
        values = activated[:, 2 * D:].reshape(TOK_DEV, HEADS, HEAD)
        unit_keys = raw_keys / jnp.sqrt(lax.optimization_barrier(jnp.sum(raw_keys * raw_keys, axis=-1, keepdims=True)) + norm_eps)
        betas = block_codes.astype(jnp.float32) * 0.25
        current_state, outputs = lax.scan(token_step, current_state, (queries, unit_keys, values, betas))
        mean_square = lax.optimization_barrier(jnp.mean(outputs * outputs, axis=-1, keepdims=True))
        normed = (outputs / jnp.sqrt(mean_square + norm_eps) * gain_heads[None]).reshape(TOK_DEV, D).astype(jnp.bfloat16)
        mixed_rows = jnp.dot(normed, w_out, preferred_element_type=jnp.float32).astype(jnp.bfloat16)
        return ((current_state, projected[TOK_DEV - 3:]), mixed_rows)
    start_state = jnp.zeros((HEADS, HEAD, HEAD), jnp.float32)
    start_rim = jnp.zeros((3, 3 * D), jnp.bfloat16)
    final_carry, mixed_blocks = lax.scan(block_step, (start_state, start_rim), (states_blocks, index_blocks, code_blocks))
    return mixed_blocks.reshape(SEQUENCE_TOKENS, D)
```

```python
import functools

import jax
import jax.numpy as jnp
from jax import lax
from jax.experimental import pallas as pl
from jax.experimental.pallas import tpu as pltpu
from jax.sharding import PartitionSpec as P

HEADS = 8
HEAD = 128
WIDTH = 1024
ROWS = 512
PATCHES = 128
CHUNK = 128
CHUNKS = ROWS // CHUNK
PAIR = 2 * HEAD
RIM = 16
HALF = HEAD // 2
SLOT = HEAD + HALF
EPS = 1e-6
MESH = pl.DeviceIdType.MESH
F32 = jnp.float32
BF16 = jnp.bfloat16


def mm(a, b):
    return jnp.dot(a.astype(BF16), b.astype(BF16), preferred_element_type=F32)


def mm_nt(a, b):
    return lax.dot_general(
        a.astype(BF16), b.astype(BF16), (((1,), (1,)), ((), ())), preferred_element_type=F32
    )


def silu(v):
    return 0.5 * v * (1.0 + jnp.tanh(0.5 * v))


def grid_of(shape):
    return lax.broadcasted_iota(jnp.int32, shape, 0), lax.broadcasted_iota(jnp.int32, shape, 1)


def level_mask(rows, cols, block):
    same = rows // (2 * block) == cols // (2 * block)
    return same & ((rows // block) % 2 == 1) & ((cols // block) % 2 == 0)


def unit_lower_inverses(lowers):
    rows, cols = grid_of((CHUNK, CHUNK))
    eye = (rows == cols).astype(F32)
    first = level_mask(rows, cols, 1)
    solved = [(eye - jnp.where(first, low, 0.0)) for low in lowers]
    block = 2
    while block < CHUNK:
        mask = level_mask(rows, cols, block)
        halves = [mm(x, jnp.where(mask, low, 0.0)) for x, low in zip(solved, lowers)]
        solved = [x - mm(half, x) for half, x in zip(halves, solved)]
        block *= 2
    return solved


def prepare_kernel(
    bytes_ref, patches_ref, rim_ref, starts_ref, codes_ref, wq_ref, wk_ref, wv_ref,
    tq_ref, tk_ref, tv_ref, move_ref, qe_ref, oe_ref, hidden, extended,
):
    pair = pl.program_id(0)

    @pl.when(pair == 0)
    def _():
        place = lax.axis_index(("outer", "inner"))
        starts = starts_ref[...]
        rows, cols = grid_of((ROWS, PATCHES))
        positions = rows + place * ROWS
        following = jnp.where(
            cols == PATCHES - 1, jnp.int32(1 << 30), pltpu.roll(jnp.broadcast_to(starts, (ROWS, PATCHES)), PATCHES - 1, 1)
        )
        chosen = (positions >= starts) & (positions < following)
        picked = mm(chosen.astype(F32), patches_ref[...])
        before = positions[:, :1] < starts[:, :1]
        picked = jnp.where(before, rim_ref[RIM - 4 : RIM - 3, :].astype(F32), picked)
        hidden[RIM:, :] = (bytes_ref[...].astype(F32) + picked).astype(BF16)
        hidden[:RIM, :] = rim_ref[...]

    def activate(w_ref, taps_ref):
        projected = jnp.dot(hidden[...], w_ref[...], preferred_element_type=F32)
        extended[...] = projected.astype(BF16).astype(F32)
        running = taps_ref[0:1, :] * extended[RIM - 3 : RIM - 3 + ROWS, :]
        for tap in range(1, 4):
            running += taps_ref[tap : tap + 1, :] * extended[RIM - 3 + tap : RIM - 3 + tap + ROWS, :]
        return silu(running)

    queries = activate(wq_ref, tq_ref)
    keys = activate(wk_ref, tk_ref)
    values = activate(wv_ref, tv_ref)
    beta_all = codes_ref[...].astype(F32) * 0.25
    rows, cols = grid_of((CHUNK, CHUNK))
    lane = lax.broadcasted_iota(jnp.int32, (ROWS, HEADS), 1)
    items = []
    for half in range(2):
        span = slice(half * HEAD, (half + 1) * HEAD)
        k = keys[:, span]
        k = k * lax.rsqrt(jnp.sum(k * k, axis=1, keepdims=True) + EPS)
        beta = jnp.sum(jnp.where(lane == 2 * pair + half, beta_all, 0.0), axis=1, keepdims=True)
        for c in range(CHUNKS):
            part = slice(c * CHUNK, (c + 1) * CHUNK)
            items.append((queries[part, span].astype(BF16), k[part], values[part, span], beta[part]))
    grams = [mm_nt(k, k) for _, k, _, _ in items]
    scores = [jnp.where(rows >= cols, mm_nt(q, k), 0.0) for q, k, _, _ in items]
    lowers = [jnp.where(rows > cols, beta * gram, 0.0) for gram, (_, _, _, beta) in zip(grams, items)]
    inverses = unit_lower_inverses(lowers)
    solved = [
        mm(x, jnp.concatenate([-beta * k, beta * v], axis=1))
        for x, (_, k, v, beta) in zip(inverses, items)
    ]
    turned = [k.T.astype(BF16) for _, k, _, _ in items]
    for half in range(2):
        state = None
        for c in range(CHUNKS):
            at = half * CHUNKS + c
            q = items[at][0]
            minus_w_u = solved[at]
            if state is None:
                fresh = minus_w_u
                result = mm(scores[at], fresh)
                state = mm(turned[at], fresh)
            else:
                fresh = minus_w_u + mm(minus_w_u[:, :HEAD], state)
                result = mm(
                    jnp.concatenate([q, scores[at].astype(BF16)], axis=1),
                    jnp.concatenate([state.astype(BF16), fresh.astype(BF16)], axis=0),
                )
                state = state + mm(turned[at], fresh)
            part = slice(c * CHUNK, (c + 1) * CHUNK)
            span = slice(half * HEAD, (half + 1) * HEAD)
            qe_ref[part, span] = (result[:, :HEAD] + q.astype(F32)).astype(BF16)
            oe_ref[part, span] = result[:, HEAD:]
        move_t = state[:, :HEAD].T
        rest_t = state[:, HEAD:].T
        move_ref[half, :HALF, :] = rest_t[:HALF].astype(BF16)
        move_ref[half, HALF : HALF + HEAD, :] = move_t.astype(BF16)
        move_ref[half, HALF + HEAD :, :] = rest_t[HALF:].astype(BF16)


def prepare(byte_states, patch_vectors, rim, patch_starts, beta_codes, w_qkv, conv_taps):
    whole = lambda *shape: pl.BlockSpec(shape, lambda p: (0,) * len(shape))
    weight = lambda part: pl.BlockSpec((WIDTH, PAIR), lambda p: (0, 4 * part + p))
    taps = lambda part: pl.BlockSpec((4, PAIR), lambda p: (0, 4 * part + p))
    return pl.pallas_call(
        prepare_kernel,
        grid=(HEADS // 2,),
        in_specs=[
            whole(ROWS, WIDTH), whole(PATCHES, WIDTH), whole(RIM, WIDTH), whole(1, PATCHES), whole(ROWS, HEADS),
            weight(0), weight(1), weight(2), taps(0), taps(1), taps(2),
        ],
        out_specs=[
            pl.BlockSpec((2, 2 * HEAD, HEAD), lambda p: (p, 0, 0)),
            pl.BlockSpec((ROWS, PAIR), lambda p: (0, p)),
            pl.BlockSpec((ROWS, PAIR), lambda p: (0, p)),
        ],
        out_shape=[
            jax.ShapeDtypeStruct((HEADS, 2 * HEAD, HEAD), BF16),
            jax.ShapeDtypeStruct((ROWS, WIDTH), BF16),
            jax.ShapeDtypeStruct((ROWS, WIDTH), F32),
        ],
        scratch_shapes=[pltpu.VMEM((RIM + ROWS, WIDTH), BF16), pltpu.VMEM((RIM + ROWS, PAIR), F32)],
        compiler_params=pltpu.CompilerParams(vmem_limit_bytes=48 << 20),
    )(byte_states, patch_vectors, rim, patch_starts, beta_codes, w_qkv, w_qkv, w_qkv, conv_taps, conv_taps, conv_taps)


def carry_kernel(
    outer_count, inner_count, move_ref, out_ref, slots, before, total, totals, states, landed,
    sem_a, recv_a, sem_b, recv_b, sem_c, recv_c,
):
    outer = lax.axis_index("outer")
    inner = lax.axis_index("inner")
    barrier = pltpu.get_barrier_semaphore()
    for step in range(1, inner_count):
        peer = lax.rem(inner + step, inner_count)
        pl.semaphore_signal(barrier, inc=1, device_id=(outer, peer), device_id_type=MESH)
    for step in range(1, outer_count):
        peer = lax.rem(outer + step, outer_count)
        pl.semaphore_signal(barrier, inc=1, device_id=(peer, inner), device_id_type=MESH)
    pl.semaphore_wait(barrier, inner_count + outer_count - 2)

    def spread(step):
        peer = lax.rem(inner + step, inner_count)
        return pltpu.make_async_remote_copy(
            src_ref=move_ref.at[peer // 2, pl.ds(pl.multiple_of((peer % 2) * HALF, HALF), SLOT)],
            dst_ref=slots.at[inner],
            send_sem=sem_a.at[peer],
            recv_sem=recv_a.at[inner],
            device_id=(outer, peer),
            device_id_type=MESH,
        )

    def spread_from(source):
        return pltpu.make_async_remote_copy(
            src_ref=slots.at[source],
            dst_ref=slots.at[source],
            send_sem=sem_a.at[source],
            recv_sem=recv_a.at[source],
            device_id=(outer, source),
            device_id_type=MESH,
        )

    for step in range(1, inner_count):
        spread(step).start()
    half = inner % 2
    slots[inner] = move_ref[inner // 2, pl.ds(pl.multiple_of(half * HALF, HALF), SLOT), :]
    moves_at = pl.multiple_of((1 - half) * HALF, HALF)
    rests_at = pl.multiple_of(half * HEAD, HALF)

    def advance(source, x):
        @pl.when(source != inner)
        def _():
            spread_from(source).wait_recv()

        before[source] = x.astype(BF16)
        moved = mm(x, slots[source, pl.ds(moves_at, HEAD), :])
        return x + moved + slots[source].astype(F32)

    x = lax.fori_loop(0, inner_count, advance, jnp.zeros((SLOT, HEAD), F32))
    total[...] = x.astype(BF16)

    def outward(peer):
        return pltpu.make_async_remote_copy(
            src_ref=total,
            dst_ref=totals.at[outer],
            send_sem=sem_b.at[peer],
            recv_sem=recv_b.at[outer],
            device_id=(peer, inner),
            device_id_type=MESH,
        )

    def outward_from(source):
        return pltpu.make_async_remote_copy(
            src_ref=total,
            dst_ref=totals.at[source],
            send_sem=sem_b.at[source],
            recv_sem=recv_b.at[source],
            device_id=(source, inner),
            device_id_type=MESH,
        )

    for step in range(1, outer_count):
        peer = outer + step

        @pl.when(peer < outer_count)
        def _():
            outward(peer).start()

    def descend(source, s):
        outward_from(source).wait_recv()
        moved = mm(s, totals[source, pl.ds(moves_at, HEAD), :])
        return s + moved + totals[source, pl.ds(rests_at, HALF), :].astype(F32)

    s = lax.fori_loop(0, outer, descend, jnp.zeros((HALF, HEAD), F32))

    def give(peer):
        return pltpu.make_async_remote_copy(
            src_ref=states.at[peer],
            dst_ref=landed.at[inner],
            send_sem=sem_c.at[peer],
            recv_sem=recv_c.at[inner],
            device_id=(outer, peer),
            device_id_type=MESH,
        )

    def give_from(source):
        return pltpu.make_async_remote_copy(
            src_ref=states.at[source],
            dst_ref=landed.at[source],
            send_sem=sem_c.at[source],
            recv_sem=recv_c.at[source],
            device_id=(outer, source),
            device_id_type=MESH,
        )

    for step in range(inner_count):
        peer = lax.rem(inner + step, inner_count)
        moved = mm(s, before[peer, pl.ds(moves_at, HEAD), :])
        at_start = s + moved + before[peer, pl.ds(rests_at, HALF), :].astype(F32)
        if step == 0:
            landed[inner] = at_start.astype(BF16)
        else:
            states[peer] = at_start.astype(BF16)
            give(peer).start()
    for step in range(1, inner_count):
        source = lax.rem(inner + step, inner_count)
        give_from(source).wait_recv()
    out_ref[...] = landed[...]
    for step in range(1, inner_count):
        peer = lax.rem(inner + step, inner_count)
        spread_from(peer).wait_send()
        give_from(peer).wait_send()
    for step in range(1, outer_count):
        peer = outer + step

        @pl.when(peer < outer_count)
        def _():
            outward(peer).wait_send()


def carry(move, outer_count, inner_count):
    dma = lambda n: pltpu.SemaphoreType.DMA((n,))
    return pl.pallas_call(
        functools.partial(carry_kernel, outer_count, inner_count),
        in_specs=[pl.BlockSpec(memory_space=pltpu.VMEM)],
        out_specs=pl.BlockSpec(memory_space=pltpu.VMEM),
        out_shape=jax.ShapeDtypeStruct((2 * HEADS, HALF, HEAD), BF16),
        scratch_shapes=[
            pltpu.VMEM((inner_count, SLOT, HEAD), BF16),
            pltpu.VMEM((inner_count, SLOT, HEAD), BF16),
            pltpu.VMEM((SLOT, HEAD), BF16),
            pltpu.VMEM((outer_count, SLOT, HEAD), BF16),
            pltpu.VMEM((inner_count, HALF, HEAD), BF16),
            pltpu.VMEM((2 * HEADS, HALF, HEAD), BF16),
            dma(inner_count), dma(inner_count), dma(outer_count), dma(outer_count), dma(inner_count), dma(inner_count),
        ],
        compiler_params=pltpu.CompilerParams(
            collective_id=0, has_side_effects=True, vmem_limit_bytes=32 << 20
        ),
    )(move)


def finish_kernel(qe_ref, oe_ref, states_ref, gain_ref, w_ref, out_ref):
    parts = []
    for head in range(HEADS):
        span = slice(head * HEAD, (head + 1) * HEAD)
        state = jnp.concatenate([states_ref[2 * head], states_ref[2 * head + 1]], axis=0)
        out = oe_ref[:, span] + mm_nt(qe_ref[:, span], state)
        mean = jnp.sum(out * out, axis=1, keepdims=True) * (1.0 / HEAD)
        parts.append((out * lax.rsqrt(mean + EPS) * gain_ref[:, span]).astype(BF16))
    normed = jnp.concatenate(parts, axis=1)
    out_ref[...] = jnp.dot(normed, w_ref[...], preferred_element_type=F32).astype(BF16)


def finish(qe, oe, states, gain, w_out):
    tile = 128
    whole = lambda *shape: pl.BlockSpec(shape, lambda p: (0,) * len(shape))
    return pl.pallas_call(
        finish_kernel,
        grid=(ROWS // tile,),
        in_specs=[
            pl.BlockSpec((tile, WIDTH), lambda p: (p, 0)),
            pl.BlockSpec((tile, WIDTH), lambda p: (p, 0)),
            whole(2 * HEADS, HALF, HEAD), whole(1, WIDTH), whole(WIDTH, WIDTH),
        ],
        out_specs=pl.BlockSpec((tile, WIDTH), lambda p: (p, 0)),
        out_shape=jax.ShapeDtypeStruct((ROWS, WIDTH), BF16),
        compiler_params=pltpu.CompilerParams(vmem_limit_bytes=32 << 20),
    )(qe, oe, states, gain, w_out)


def shifted(value, axis, steps):
    count = lax.axis_size(axis)
    return lax.ppermute(value, axis, [(source, source + steps) for source in range(count - steps)])


def local(byte_states, patch_vectors, patch_starts, beta_codes, w_qkv, conv_taps, norm_gain, w_out):
    place = lax.axis_index(("outer", "inner"))
    last = jnp.arange(ROWS - 3, ROWS, dtype=jnp.int32) + place * ROWS
    index = jnp.sum((patch_starts[None, :] <= last[:, None]).astype(jnp.int32), axis=1) - 1
    fetched = jnp.take(patch_vectors, index, axis=0)
    rim = (byte_states[ROWS - 3 :].astype(F32) + fetched.astype(F32)).astype(BF16)
    rim = jnp.concatenate([jnp.zeros((RIM - 4, WIDTH), BF16), patch_vectors[PATCHES - 1 :], rim], axis=0)
    rim = shifted(rim, ("outer", "inner"), 1)
    move, qe, oe = prepare(
        byte_states, patch_vectors, rim, patch_starts.reshape(1, PATCHES), beta_codes, w_qkv, conv_taps
    )
    states = carry(move, lax.axis_size("outer"), lax.axis_size("inner"))
    return finish(qe, oe, states, norm_gain.reshape(1, WIDTH), w_out)


def solution(mesh):
    in_specs = (
        P(("outer", "inner"), None),
        P(("outer", "inner"), None),
        P(("outer", "inner")),
        P(("outer", "inner"), None),
        P(),
        P(),
        P(),
        P(),
    )
    out_specs = P(("outer", "inner"), None)
    return jax.shard_map(local, mesh=mesh, in_specs=in_specs, out_specs=out_specs, check_vma=False)
```

```python
import functools

import jax
import jax.numpy as jnp
from jax import lax
from jax.experimental import pallas as pl
from jax.experimental.pallas import tpu as pltpu
from jax.sharding import PartitionSpec as P

HEADS = 8
HEAD = 128
WIDTH = 1024
ROWS = 512
PATCHES = 128
CHUNK = 128
RIM = 16
HALF_ROWS = ROWS // 2
GROUP = HEADS // 2
COLS = GROUP * HEAD
HALF = HEAD // 2
SLOT = HEAD + HALF
EPS = 1e-6
MESH = pl.DeviceIdType.MESH
F32 = jnp.float32
BF16 = jnp.bfloat16


def mm(a, b):
    return jnp.dot(a.astype(BF16), b.astype(BF16), preferred_element_type=F32)


def mm_nt(a, b):
    return lax.dot_general(
        a.astype(BF16), b.astype(BF16), (((1,), (1,)), ((), ())), preferred_element_type=F32
    )


def silu(v):
    return 0.5 * v * (1.0 + jnp.tanh(0.5 * v))


def grid_of(shape):
    return lax.broadcasted_iota(jnp.int32, shape, 0), lax.broadcasted_iota(jnp.int32, shape, 1)


def level_mask(rows, cols, block):
    same = rows // (2 * block) == cols // (2 * block)
    return same & ((rows // block) % 2 == 1) & ((cols // block) % 2 == 0)


def unit_lower_inverses(lowers):
    rows, cols = grid_of((CHUNK, CHUNK))
    eye = (rows == cols).astype(F32)
    first = level_mask(rows, cols, 1)
    solved = [(eye - jnp.where(first, low, 0.0)) for low in lowers]
    block = 2
    while block < CHUNK:
        mask = level_mask(rows, cols, block)
        halves = [mm(x, jnp.where(mask, low, 0.0)) for x, low in zip(solved, lowers)]
        solved = [x - mm(half, x) for half, x in zip(halves, solved)]
        block *= 2
    return solved


def joined(earlier, later):
    return earlier + later + mm(earlier, later[:HEAD])


def kernel(
    outer_count, inner_count,
    bytes_hbm, patches_hbm, starts_ref, codes_ref, w_hbm, taps_ref, gain_ref, wout_hbm, out_ref,
    hidden, patches, weights, wout, rim_out, rim_in, betas, ext_k, ext_v, ext_q, unit_keys, solved_ref,
    firsts, pairs, moves, slots, before, tree, total, totals, states, landed, qe, oe,
    sem_in, sem_rim, sem_a, recv_a, sem_b, recv_b, sem_c, recv_c,
):
    outer = lax.axis_index("outer")
    inner = lax.axis_index("inner")
    place = outer * inner_count + inner
    devices = outer_count * inner_count

    loads = [
        pltpu.make_async_copy(bytes_hbm, hidden.at[pl.ds(RIM, ROWS)], sem_in.at[0]),
        pltpu.make_async_copy(patches_hbm, patches, sem_in.at[1]),
    ]
    for at, (part, group) in enumerate([(1, 0), (2, 0), (1, 1), (2, 1), (0, 0), (0, 1)]):
        loads.append(
            pltpu.make_async_copy(
                w_hbm.at[:, pl.ds(part * WIDTH + group * COLS, COLS)], weights.at[part, group], sem_in.at[2 + at]
            )
        )
    loads.append(pltpu.make_async_copy(wout_hbm, wout, sem_in.at[8]))
    for load in loads:
        load.start()

    barrier = pltpu.get_barrier_semaphore()

    def device_at(index):
        index = lax.rem(index + devices, devices)
        return (index // inner_count, lax.rem(index, inner_count))

    following, preceding = device_at(place + 1), device_at(place - 1)
    for neighbour in (following, preceding):
        pl.semaphore_signal(barrier, inc=1, device_id=neighbour, device_id_type=MESH)
    for step in range(1, inner_count):
        peer = lax.rem(inner + step, inner_count)
        pl.semaphore_signal(barrier, inc=1, device_id=(outer, peer), device_id_type=MESH)
    for step in range(1, outer_count):
        peer = lax.rem(outer + step, outer_count)
        pl.semaphore_signal(barrier, inc=1, device_id=(peer, inner), device_id_type=MESH)

    starts = starts_ref[...]
    rows, cols = grid_of((ROWS, PATCHES))
    positions = rows + place * ROWS
    next_starts = jnp.where(cols == PATCHES - 1, jnp.int32(1 << 30), pltpu.roll(jnp.broadcast_to(starts, (ROWS, PATCHES)), PATCHES - 1, 1))
    chosen = ((positions >= starts) & (positions < next_starts)).astype(BF16)
    open_rows = positions[:, :1] < starts[:, :1]
    for group in range(2):
        turned = codes_ref[group * GROUP : (group + 1) * GROUP, :].astype(F32) * 0.25
        betas[group] = turned.T
    loads[0].wait()
    loads[1].wait()
    picked = jnp.dot(chosen, patches[...], preferred_element_type=F32)
    hidden[RIM:, :] = (hidden[RIM:, :].astype(F32) + picked).astype(BF16)
    rim_rows, _ = grid_of((RIM, WIDTH))
    rim_out[...] = jnp.where(
        rim_rows == RIM - 4, patches[PATCHES - 1 :, :].astype(F32), hidden[ROWS:, :].astype(F32)
    ).astype(BF16)
    pl.semaphore_wait(barrier, inner_count + outer_count)
    rim_copy = pltpu.make_async_remote_copy(
        src_ref=rim_out, dst_ref=rim_in, send_sem=sem_rim.at[0], recv_sem=sem_rim.at[1],
        device_id=following, device_id_type=MESH,
    )
    rim_copy.start()
    for load in loads[2:6]:
        load.wait()
    rim_copy.wait_recv()
    rim = jnp.where(place > 0, rim_in[...].astype(F32), 0.0)
    hidden[:RIM, :] = rim.astype(BF16)
    filled = hidden[RIM:, :].astype(F32)
    hidden[RIM:, :] = jnp.where(open_rows, filled + rim[RIM - 4 : RIM - 3, :], filled).astype(BF16)

    def activate(part, row_half, group, ext):
        here = hidden[pl.ds(pl.multiple_of(row_half * HALF_ROWS, HALF_ROWS), HALF_ROWS + RIM), :]
        projected = jnp.dot(here, weights[part, group], preferred_element_type=F32)
        ext[...] = projected.astype(BF16).astype(F32)
        lanes = pl.ds(pl.multiple_of(part * WIDTH + group * COLS, COLS), COLS)
        running = taps_ref[0:1, lanes] * ext[RIM - 3 : RIM - 3 + HALF_ROWS, :]
        for tap in range(1, 4):
            running += taps_ref[tap : tap + 1, lanes] * ext[RIM - 3 + tap : RIM - 3 + tap + HALF_ROWS, :]
        return silu(running)

    tile_rows, tile_cols = grid_of((CHUNK, CHUNK))

    def spread(role):
        return pltpu.make_async_remote_copy(
            src_ref=moves.at[role], dst_ref=slots.at[inner], send_sem=sem_a.at[role], recv_sem=recv_a.at[inner],
            device_id=(outer, role), device_id_type=MESH,
        )

    def spread_from(source):
        return pltpu.make_async_remote_copy(
            src_ref=moves.at[source], dst_ref=slots.at[source], send_sem=sem_a.at[source], recv_sem=recv_a.at[source],
            device_id=(outer, source), device_id_type=MESH,
        )

    def critical(step, _):
        row_half, group = 1 - step // 2, lax.rem(step, 2)
        keys = activate(1, row_half, group, ext_k)
        values = activate(2, row_half, group, ext_v)
        beta = betas[group, pl.ds(pl.multiple_of(row_half * HALF_ROWS, HALF_ROWS), HALF_ROWS), :]
        items = []
        for head in range(GROUP):
            span = slice(head * HEAD, (head + 1) * HEAD)
            k = keys[:, span]
            k = k * lax.rsqrt(jnp.sum(k * k, axis=1, keepdims=True) + EPS)
            unit_keys[row_half, group, head] = k.astype(BF16)
            for c in range(2):
                part = slice(c * CHUNK, (c + 1) * CHUNK)
                items.append((k[part], values[part, span], beta[part, head : head + 1]))
        lowers = [jnp.where(tile_rows > tile_cols, beta * mm_nt(k, k), 0.0) for k, _, beta in items]
        inverses = unit_lower_inverses(lowers)
        solved = [
            mm(x, jnp.concatenate([-beta * k, beta * v], axis=1)).astype(BF16)
            for x, (k, v, beta) in zip(inverses, items)
        ]
        parts = [mm(k.T, s) for (k, _, _), s in zip(items, solved)]
        for head in range(GROUP):
            first, second = parts[2 * head], parts[2 * head + 1]
            for c in range(2):
                solved_ref[row_half, group, head, c] = solved[2 * head + c]
            firsts[row_half, group, head] = first.astype(BF16)
            pairs[row_half, group, head] = first + second + mm(second[:, :HEAD], first)

        @pl.when(row_half == 0)
        def _():
            for head in range(GROUP):
                early, late = pairs[0, group, head], pairs[1, group, head]
                whole = early + late + mm(late[:, :HEAD], early)
                move = whole[:, :HEAD].T.astype(BF16)
                rest = whole[:, HEAD:].T.astype(BF16)
                for half in range(2):
                    role = (group * GROUP + head) * 2 + half
                    moves[role, :HEAD, :] = move
                    moves[role, HEAD:, :] = rest[half * HALF : (half + 1) * HALF]

            for at in range(2 * GROUP):
                role = group * 2 * GROUP + at

                @pl.when(role != inner)
                def _():
                    spread(role).start()

                @pl.when(role == inner)
                def _():
                    slots[inner] = moves[role]

        return 0

    lax.fori_loop(0, 4, critical, 0)

    for load in loads[6:8]:
        load.wait()

    def deferred(step, _):
        row_half, group = step // 2, lax.rem(step, 2)
        queries = activate(0, row_half, group, ext_q)
        late = (row_half == 1).astype(F32)
        for head in range(GROUP):
            span = slice(head * HEAD, (head + 1) * HEAD)
            k = unit_keys[row_half, group, head]
            first = firsts[row_half, group, head]
            state_a = pairs[0, group, head] * late
            state_b = state_a + first.astype(F32) + mm(first[:, :HEAD], state_a)
            for c, state in enumerate((state_a, state_b)):
                part = slice(c * CHUNK, (c + 1) * CHUNK)
                q = queries[part, span]
                score = jnp.where(tile_rows >= tile_cols, mm_nt(q, k[part]), 0.0)
                base = mm(score, solved_ref[row_half, group, head, c])
                reach = base[:, :HEAD] + q
                result = mm(reach, state)
                to = pl.ds(pl.multiple_of(row_half * HALF_ROWS + c * CHUNK, CHUNK), CHUNK)
                qe[group, head, to, :] = (reach + result[:, :HEAD]).astype(BF16)
                oe[group, head, to, :] = base[:, HEAD:] + result[:, HEAD:]
        return 0

    lax.fori_loop(0, 4, deferred, 0)

    for step in range(1, inner_count):
        spread_from(lax.rem(inner + step, inner_count)).wait_recv()
    for at in range(inner_count // 2):
        tree[at] = joined(slots[2 * at].astype(F32), slots[2 * at + 1].astype(F32)).astype(BF16)
    count = inner_count // 4
    while count:
        for at in range(count):
            tree[at] = joined(tree[2 * at].astype(F32), tree[2 * at + 1].astype(F32)).astype(BF16)
        count //= 2
    total[...] = tree[0]

    def outward(peer):
        return pltpu.make_async_remote_copy(
            src_ref=total, dst_ref=totals.at[outer], send_sem=sem_b.at[peer], recv_sem=recv_b.at[outer],
            device_id=(peer, inner), device_id_type=MESH,
        )

    def outward_from(source):
        return pltpu.make_async_remote_copy(
            src_ref=total, dst_ref=totals.at[source], send_sem=sem_b.at[source], recv_sem=recv_b.at[source],
            device_id=(source, inner), device_id_type=MESH,
        )

    for step in range(1, outer_count):
        peer = outer + step

        @pl.when(peer < outer_count)
        def _():
            outward(peer).start()

    running = jnp.zeros((SLOT, HEAD), F32)
    for at in range(inner_count):
        before[at] = running.astype(BF16)
        if at < inner_count - 1:
            running = joined(running, slots[at].astype(F32))

    def descend(source, s):
        outward_from(source).wait_recv()
        return s + mm(s, totals[source, :HEAD, :]) + totals[source, HEAD:, :].astype(F32)

    s = lax.fori_loop(0, outer, descend, jnp.zeros((HALF, HEAD), F32))

    def give(peer):
        return pltpu.make_async_remote_copy(
            src_ref=states.at[peer], dst_ref=landed.at[inner], send_sem=sem_c.at[peer], recv_sem=recv_c.at[inner],
            device_id=(outer, peer), device_id_type=MESH,
        )

    def give_from(source):
        return pltpu.make_async_remote_copy(
            src_ref=states.at[source], dst_ref=landed.at[source], send_sem=sem_c.at[source],
            recv_sem=recv_c.at[source], device_id=(outer, source), device_id_type=MESH,
        )

    for step in range(1, inner_count + 1):
        peer = lax.rem(inner + step, inner_count)
        at_start = (s + mm(s, before[peer, :HEAD, :]) + before[peer, HEAD:, :].astype(F32)).astype(BF16)
        if step == inner_count:
            landed[inner] = at_start
        else:
            states[peer] = at_start
            give(peer).start()
    loads[8].wait()
    for step in range(1, inner_count):
        give_from(lax.rem(inner + step, inner_count)).wait_recv()

    def finish(tile, _):
        at = pl.ds(pl.multiple_of(tile * CHUNK, CHUNK), CHUNK)
        parts = []
        for head in range(HEADS):
            state = jnp.concatenate([landed[2 * head], landed[2 * head + 1]], axis=0)
            group, inside = head // GROUP, head % GROUP
            result = oe[group, inside, at, :] + mm_nt(qe[group, inside, at, :], state)
            mean = jnp.sum(result * result, axis=1, keepdims=True) * (1.0 / HEAD)
            gain = gain_ref[:, head * HEAD : (head + 1) * HEAD]
            parts.append((result * lax.rsqrt(mean + EPS) * gain).astype(BF16))
        normed = jnp.concatenate(parts, axis=1)
        out_ref[at, :] = jnp.dot(normed, wout[...], preferred_element_type=F32).astype(BF16)
        return 0

    lax.fori_loop(0, ROWS // CHUNK, finish, 0)

    rim_copy.wait_send()
    for step in range(1, inner_count):
        peer = lax.rem(inner + step, inner_count)
        spread_from(peer).wait_send()
        give_from(peer).wait_send()
    for step in range(1, outer_count):
        peer = outer + step

        @pl.when(peer < outer_count)
        def _():
            outward(peer).wait_send()


def local(byte_states, patch_vectors, patch_starts, beta_codes, w_qkv, conv_taps, norm_gain, w_out):
    outer_count, inner_count = lax.axis_size("outer"), lax.axis_size("inner")
    dma = lambda *n: pltpu.SemaphoreType.DMA(n)
    vmem = lambda *shape: pltpu.VMEM(shape, BF16)
    wide = lambda *shape: pltpu.VMEM(shape, F32)
    here, far = pl.BlockSpec(memory_space=pltpu.VMEM), pl.BlockSpec(memory_space=pl.ANY)
    return pl.pallas_call(
        functools.partial(kernel, outer_count, inner_count),
        in_specs=[far, far, here, here, far, here, here, far],
        out_specs=here,
        out_shape=jax.ShapeDtypeStruct((ROWS, WIDTH), BF16),
        scratch_shapes=[
            vmem(RIM + ROWS, WIDTH),
            vmem(PATCHES, WIDTH),
            vmem(3, 2, WIDTH, COLS),
            vmem(WIDTH, WIDTH),
            vmem(RIM, WIDTH),
            vmem(RIM, WIDTH),
            wide(2, ROWS, GROUP),
            wide(RIM + HALF_ROWS, COLS),
            wide(RIM + HALF_ROWS, COLS),
            wide(RIM + HALF_ROWS, COLS),
            vmem(2, 2, GROUP, HALF_ROWS, HEAD),
            vmem(2, 2, GROUP, 2, CHUNK, 2 * HEAD),
            vmem(2, 2, GROUP, HEAD, 2 * HEAD),
            wide(2, 2, GROUP, HEAD, 2 * HEAD),
            vmem(inner_count, SLOT, HEAD),
            vmem(inner_count, SLOT, HEAD),
            vmem(inner_count, SLOT, HEAD),
            vmem(inner_count // 2, SLOT, HEAD),
            vmem(SLOT, HEAD),
            vmem(outer_count, SLOT, HEAD),
            vmem(inner_count, HALF, HEAD),
            vmem(inner_count, HALF, HEAD),
            vmem(2, GROUP, ROWS, HEAD),
            wide(2, GROUP, ROWS, HEAD),
            dma(9), dma(2),
            dma(inner_count), dma(inner_count), dma(outer_count), dma(outer_count), dma(inner_count), dma(inner_count),
        ],
        compiler_params=pltpu.CompilerParams(
            collective_id=0, has_side_effects=True, vmem_limit_bytes=63 << 20
        ),
    )(
        byte_states, patch_vectors, patch_starts.reshape(1, PATCHES), beta_codes.T, w_qkv, conv_taps,
        norm_gain.reshape(1, WIDTH), w_out,
    )


def solution(mesh):
    in_specs = (
        P(("outer", "inner"), None),
        P(("outer", "inner"), None),
        P(("outer", "inner")),
        P(("outer", "inner"), None),
        P(),
        P(),
        P(),
        P(),
    )
    out_specs = P(("outer", "inner"), None)
    return jax.shard_map(local, mesh=mesh, in_specs=in_specs, out_specs=out_specs, check_vma=False)
```

```python
import functools

import jax
import jax.numpy as jnp
from jax import lax
from jax.experimental import pallas as pl
from jax.experimental.pallas import tpu as pltpu
from jax.sharding import PartitionSpec as P

HEADS = 8
HEAD = 128
WIDTH = 1024
ROWS = 512
PATCHES = 128
CHUNK = 128
FINISH = 256
PIECES = 4
RIM = 16
HALF_ROWS = ROWS // 2
GROUP = HEADS // 2
COLS = GROUP * HEAD
HALF = HEAD // 2
SLOT = HEAD + HALF
EPS = 1e-6
MESH = pl.DeviceIdType.MESH
F32 = jnp.float32
BF16 = jnp.bfloat16


def mm(a, b):
    return jnp.dot(a.astype(BF16), b.astype(BF16), preferred_element_type=F32)


def mm_nt(a, b):
    return lax.dot_general(
        a.astype(BF16), b.astype(BF16), (((1,), (1,)), ((), ())), preferred_element_type=F32
    )


def silu(v):
    return 0.5 * v * (1.0 + jnp.tanh(0.5 * v))


def grid_of(shape):
    return lax.broadcasted_iota(jnp.int32, shape, 0), lax.broadcasted_iota(jnp.int32, shape, 1)


def level_mask(rows, cols, block):
    same = rows // (2 * block) == cols // (2 * block)
    return same & ((rows // block) % 2 == 1) & ((cols // block) % 2 == 0)


def unit_lower_inverses(lowers):
    rows, cols = grid_of((CHUNK, CHUNK))
    eye = (rows == cols).astype(F32)
    first = level_mask(rows, cols, 1)
    solved = [(eye - jnp.where(first, low, 0.0)) for low in lowers]
    block = 2
    while block < CHUNK:
        mask = level_mask(rows, cols, block)
        halves = [mm(x, jnp.where(mask, low, 0.0)) for x, low in zip(solved, lowers)]
        solved = [x - mm(half, x) for half, x in zip(halves, solved)]
        block *= 2
    return solved


def halves_of(x):
    high = x.astype(BF16)
    return high, (x - high.astype(F32)).astype(BF16)


def gram_of(k):
    high, low = halves_of(k)
    crossed = mm_nt(jnp.concatenate([high, low], axis=1), jnp.concatenate([low, high], axis=1))
    return mm_nt(high, high) + crossed


def role_of(inner):
    z, x = inner // 4, inner % 4
    return (x + z) % 2 * HEADS + z * 2 + x // 2


def inner_of(role):
    z = role % HEADS // 2
    return z * 4 + role % 2 * 2 + (role // HEADS + z) % 2


def joined(earlier, later):
    return earlier + later + mm(earlier, later[:HEAD])


def kernel(
    outer_count, inner_count,
    bytes_hbm, patches_hbm, starts_ref, codes_ref, w_hbm, taps_ref, gain_ref, wout_hbm, out_ref,
    hidden, patches, weights, wout, rim_out, rim_in, betas, ext_k, ext_v, ext_q, unit_keys, solved_ref,
    firsts, pairs, moves, slots, before, tree, total, totals, states, landed, qe, oe,
    mixed, sem_in, sem_out, sem_rim, sem_a, recv_a, sem_b, recv_b, sem_c, recv_c,
):
    outer = lax.axis_index("outer")
    inner = lax.axis_index("inner")
    place = outer * inner_count + inner
    mine = role_of(inner)
    devices = outer_count * inner_count

    loads = [
        pltpu.make_async_copy(bytes_hbm, hidden.at[pl.ds(RIM, ROWS)], sem_in.at[0]),
        pltpu.make_async_copy(patches_hbm, patches, sem_in.at[1]),
    ]
    for at, (part, group) in enumerate([(1, 0), (2, 0), (1, 1), (2, 1), (0, 0), (0, 1)]):
        loads.append(
            pltpu.make_async_copy(
                w_hbm.at[:, pl.ds(part * WIDTH + group * COLS, COLS)], weights.at[part, group], sem_in.at[2 + at]
            )
        )
    loads.append(pltpu.make_async_copy(wout_hbm, wout, sem_in.at[8]))
    for load in loads[:2]:
        load.start()

    barrier = pltpu.get_barrier_semaphore()

    def device_at(index):
        index = lax.rem(index + devices, devices)
        return (index // inner_count, lax.rem(index, inner_count))

    following, preceding = device_at(place + 1), device_at(place - 1)
    for neighbour in (following, preceding):
        pl.semaphore_signal(barrier, inc=1, device_id=neighbour, device_id_type=MESH)
    for step in range(1, inner_count):
        peer = lax.rem(inner + step, inner_count)
        pl.semaphore_signal(barrier, inc=1, device_id=(outer, peer), device_id_type=MESH)
    for step in range(1, outer_count):
        peer = lax.rem(outer + step, outer_count)
        pl.semaphore_signal(barrier, inc=1, device_id=(peer, inner), device_id_type=MESH)

    for load in loads[2:]:
        load.start()

    starts = starts_ref[...]
    rows, cols = grid_of((ROWS, PATCHES))
    positions = rows + place * ROWS
    next_starts = jnp.where(cols == PATCHES - 1, jnp.int32(1 << 30), pltpu.roll(jnp.broadcast_to(starts, (ROWS, PATCHES)), PATCHES - 1, 1))
    chosen = ((positions >= starts) & (positions < next_starts)).astype(BF16)
    open_rows = positions[:, :1] < starts[:, :1]
    for group in range(2):
        turned = codes_ref[group * GROUP : (group + 1) * GROUP, :].astype(F32) * 0.25
        betas[group] = turned.T
    loads[0].wait()
    loads[1].wait()
    tail = hidden[ROWS:, :].astype(F32) + jnp.dot(chosen[ROWS - RIM :], patches[...], preferred_element_type=F32)
    rim_rows, _ = grid_of((RIM, WIDTH))
    rim_out[...] = jnp.where(rim_rows == RIM - 4, patches[PATCHES - 1 :, :].astype(F32), tail).astype(BF16)
    pl.semaphore_wait(barrier, inner_count + outer_count)
    rim_copy = pltpu.make_async_remote_copy(
        src_ref=rim_out, dst_ref=rim_in, send_sem=sem_rim.at[0], recv_sem=sem_rim.at[1],
        device_id=following, device_id_type=MESH,
    )
    rim_copy.start()
    picked = jnp.dot(chosen, patches[...], preferred_element_type=F32)
    hidden[RIM:, :] = (hidden[RIM:, :].astype(F32) + picked).astype(BF16)
    for load in loads[2:6]:
        load.wait()
    rim_copy.wait_recv()
    rim = jnp.where(place > 0, rim_in[...].astype(F32), 0.0)
    hidden[:RIM, :] = rim.astype(BF16)
    can_be_open = pl.ds(RIM, ROWS - PATCHES)
    filled = hidden[can_be_open, :].astype(F32)
    hidden[can_be_open, :] = jnp.where(
        open_rows[: ROWS - PATCHES], filled + rim[RIM - 4 : RIM - 3, :], filled
    ).astype(BF16)

    def activate(part, row_half, group, ext):
        here = hidden[pl.ds(pl.multiple_of(row_half * HALF_ROWS, HALF_ROWS), HALF_ROWS + RIM), :]
        projected = jnp.dot(here, weights[part, group], preferred_element_type=F32)
        ext[...] = projected.astype(BF16).astype(F32)
        lanes = pl.ds(pl.multiple_of(part * WIDTH + group * COLS, COLS), COLS)
        running = taps_ref[0:1, lanes] * ext[RIM - 3 : RIM - 3 + HALF_ROWS, :]
        for tap in range(1, 4):
            running += taps_ref[tap : tap + 1, lanes] * ext[RIM - 3 + tap : RIM - 3 + tap + HALF_ROWS, :]
        return silu(running)

    tile_rows, tile_cols = grid_of((CHUNK, CHUNK))

    def spread(role):
        return pltpu.make_async_remote_copy(
            src_ref=moves.at[role], dst_ref=slots.at[inner], send_sem=sem_a.at[role], recv_sem=recv_a.at[inner],
            device_id=(outer, inner_of(role)), device_id_type=MESH,
        )

    def spread_from(source):
        return pltpu.make_async_remote_copy(
            src_ref=moves.at[role_of(source)], dst_ref=slots.at[source], send_sem=sem_a.at[role_of(source)],
            recv_sem=recv_a.at[source], device_id=(outer, source), device_id_type=MESH,
        )

    def critical(step, _):
        row_half, group = 1 - lax.rem(step, 2), step // 2
        keys = activate(1, row_half, group, ext_k)
        values = activate(2, row_half, group, ext_v)
        beta = betas[group, pl.ds(pl.multiple_of(row_half * HALF_ROWS, HALF_ROWS), HALF_ROWS), :]
        items = []
        for head in range(GROUP):
            span = slice(head * HEAD, (head + 1) * HEAD)
            k = keys[:, span]
            k = k * lax.rsqrt(jnp.sum(k * k, axis=1, keepdims=True) + EPS)
            unit_keys[row_half, group, head] = k.astype(BF16)
            for c in range(2):
                part = slice(c * CHUNK, (c + 1) * CHUNK)
                items.append((k[part], values[part, span], beta[part, head : head + 1]))
        lowers = [jnp.where(tile_rows > tile_cols, beta * gram_of(k), 0.0) for k, _, beta in items]
        inverses = unit_lower_inverses(lowers)
        sides = [jnp.concatenate([-beta * k, beta * v], axis=1) for k, v, beta in items]
        rough = [mm(x, side).astype(BF16) for x, side in zip(inverses, sides)]
        missed = [
            side - z.astype(F32) - mm(jnp.concatenate(halves_of(low), axis=1), jnp.concatenate([z, z], axis=0))
            for z, low, side in zip(rough, lowers, sides)
        ]
        solved = [(z.astype(F32) + mm(x, left)).astype(BF16) for z, x, left in zip(rough, inverses, missed)]
        parts = [mm(k.astype(BF16).T, s) for (k, _, _), s in zip(items, solved)]
        for head in range(GROUP):
            first, second = parts[2 * head], parts[2 * head + 1]
            for c in range(2):
                solved_ref[row_half, group, head, c] = solved[2 * head + c]
            firsts[row_half, group, head] = first.astype(BF16)
            pairs[row_half, group, head] = first + second + mm(second[:, :HEAD], first)

        @pl.when(row_half == 0)
        def _():
            for head in range(GROUP):
                early, late = pairs[0, group, head], pairs[1, group, head]
                whole = early + late + mm(late[:, :HEAD], early)
                flipped = whole.astype(BF16).T
                move, rest = flipped[:HEAD], flipped[HEAD:]
                for half in range(2):
                    role = (group * GROUP + head) * 2 + half
                    moves[role, :HEAD, :] = move
                    moves[role, HEAD:, :] = rest[half * HALF : (half + 1) * HALF]

            for at in range(2 * GROUP):
                role = group * 2 * GROUP + at

                @pl.when(role != mine)
                def _():
                    spread(role).start()

                @pl.when(role == mine)
                def _():
                    slots[inner] = moves[role]

        return 0

    lax.fori_loop(0, 4, critical, 0)

    for load in loads[6:8]:
        load.wait()

    def deferred(step, _):
        row_half, group = step // 2, lax.rem(step, 2)
        queries = activate(0, row_half, group, ext_q)
        late = (row_half == 1).astype(F32)
        for head in range(GROUP):
            span = slice(head * HEAD, (head + 1) * HEAD)
            k = unit_keys[row_half, group, head]
            first = firsts[row_half, group, head]
            state_a = pairs[0, group, head] * late
            state_b = state_a + first.astype(F32) + mm(first[:, :HEAD], state_a)
            for c, state in enumerate((state_a, state_b)):
                part = slice(c * CHUNK, (c + 1) * CHUNK)
                q = queries[part, span]
                score = jnp.where(tile_rows >= tile_cols, mm_nt(q, k[part]), 0.0)
                base = mm(score, solved_ref[row_half, group, head, c])
                reach = base[:, :HEAD] + q
                result = mm(reach, state)
                to = pl.ds(pl.multiple_of(row_half * HALF_ROWS + c * CHUNK, CHUNK), CHUNK)
                qe[group, head, to, :] = (reach + result[:, :HEAD]).astype(BF16)
                oe[group, head, to, :] = base[:, HEAD:] + result[:, HEAD:]
        return 0

    lax.fori_loop(0, 4, deferred, 0)

    for step in range(1, inner_count):
        spread_from(lax.rem(inner + step, inner_count)).wait_recv()
    for at in range(inner_count // 2):
        tree[at] = joined(slots[2 * at].astype(F32), slots[2 * at + 1].astype(F32)).astype(BF16)
    count = inner_count // 4
    while count:
        for at in range(count):
            tree[at] = joined(tree[2 * at].astype(F32), tree[2 * at + 1].astype(F32)).astype(BF16)
        count //= 2
    total[...] = tree[0]

    def outward(peer):
        return pltpu.make_async_remote_copy(
            src_ref=total, dst_ref=totals.at[outer], send_sem=sem_b.at[peer], recv_sem=recv_b.at[outer],
            device_id=(peer, inner), device_id_type=MESH,
        )

    def outward_from(source):
        return pltpu.make_async_remote_copy(
            src_ref=total, dst_ref=totals.at[source], send_sem=sem_b.at[source], recv_sem=recv_b.at[source],
            device_id=(source, inner), device_id_type=MESH,
        )

    for step in range(1, outer_count):
        peer = outer + step

        @pl.when(peer < outer_count)
        def _():
            outward(peer).start()

    running = jnp.zeros((SLOT, HEAD), F32)
    for at in range(inner_count):
        before[at] = running.astype(BF16)
        if at < inner_count - 1:
            running = joined(running, slots[at].astype(F32))

    def descend(source, s):
        outward_from(source).wait_recv()
        return s + mm(s, totals[source, :HEAD, :]) + totals[source, HEAD:, :].astype(F32)

    s = lax.fori_loop(0, outer, descend, jnp.zeros((HALF, HEAD), F32))

    def give(peer):
        return pltpu.make_async_remote_copy(
            src_ref=states.at[peer], dst_ref=landed.at[mine], send_sem=sem_c.at[peer], recv_sem=recv_c.at[mine],
            device_id=(outer, peer), device_id_type=MESH,
        )

    def give_from(source):
        return pltpu.make_async_remote_copy(
            src_ref=states.at[source], dst_ref=landed.at[role_of(source)], send_sem=sem_c.at[source],
            recv_sem=recv_c.at[role_of(source)], device_id=(outer, source), device_id_type=MESH,
        )

    for step in range(1, inner_count + 1):
        peer = lax.rem(inner + step, inner_count)
        at_start = (s + mm(s, before[peer, :HEAD, :]) + before[peer, HEAD:, :].astype(F32)).astype(BF16)
        if step == inner_count:
            landed[mine] = at_start
        else:
            states[peer] = at_start
            give(peer).start()
    loads[8].wait()
    for step in range(1, inner_count):
        give_from(lax.rem(inner + step, inner_count)).wait_recv()

    written = []
    for tile in range(ROWS // FINISH):
        at = slice(tile * FINISH, (tile + 1) * FINISH)
        parts = []
        for head in range(HEADS):
            state = jnp.concatenate([landed[2 * head], landed[2 * head + 1]], axis=0)
            group, inside = head // GROUP, head % GROUP
            result = oe[group, inside, at, :] + mm_nt(qe[group, inside, at, :], state)
            mean = jnp.sum(result * result, axis=1, keepdims=True) * (1.0 / HEAD)
            gain = gain_ref[:, head * HEAD : (head + 1) * HEAD]
            parts.append((result * lax.rsqrt(mean + EPS) * gain).astype(BF16))
        normed = jnp.concatenate(parts, axis=1)
        mixed[at, :] = jnp.dot(normed, wout[...], preferred_element_type=F32).astype(BF16)
        written.append(pltpu.make_async_copy(mixed.at[at], out_ref.at[at], sem_out.at[tile]))
        written[-1].start()

    for copy in written:
        copy.wait()
    rim_copy.wait_send()
    for step in range(1, inner_count):
        peer = lax.rem(inner + step, inner_count)
        spread_from(peer).wait_send()
        give_from(peer).wait_send()
    for step in range(1, outer_count):
        peer = outer + step

        @pl.when(peer < outer_count)
        def _():
            outward(peer).wait_send()


def copy_kernel(from_ref, to_ref, held, sem_from, sem_to):
    pieces = [pl.ds(at * (ROWS // PIECES), ROWS // PIECES) for at in range(PIECES)]
    arriving = [pltpu.make_async_copy(from_ref.at[p], held.at[p], sem_from.at[at]) for at, p in enumerate(pieces)]
    leaving = [pltpu.make_async_copy(held.at[p], to_ref.at[p], sem_to.at[at]) for at, p in enumerate(pieces)]
    for copy in arriving:
        copy.start()
    for first, second in zip(arriving, leaving):
        first.wait()
        second.start()
    for copy in leaving:
        copy.wait()


def local(byte_states, patch_vectors, patch_starts, beta_codes, w_qkv, conv_taps, norm_gain, w_out):
    outer_count, inner_count = lax.axis_size("outer"), lax.axis_size("inner")
    dma = lambda *n: pltpu.SemaphoreType.DMA(n)
    vmem = lambda *shape: pltpu.VMEM(shape, BF16)
    wide = lambda *shape: pltpu.VMEM(shape, F32)
    here, far = pl.BlockSpec(memory_space=pltpu.VMEM), pl.BlockSpec(memory_space=pl.ANY)
    mixed = pl.pallas_call(
        functools.partial(kernel, outer_count, inner_count),
        in_specs=[far, far, here, here, far, here, here, far],
        out_specs=far,
        out_shape=jax.ShapeDtypeStruct((ROWS, WIDTH), BF16),
        scratch_shapes=[
            vmem(RIM + ROWS, WIDTH),
            vmem(PATCHES, WIDTH),
            vmem(3, 2, WIDTH, COLS),
            vmem(WIDTH, WIDTH),
            vmem(RIM, WIDTH),
            vmem(RIM, WIDTH),
            wide(2, ROWS, GROUP),
            wide(RIM + HALF_ROWS, COLS),
            wide(RIM + HALF_ROWS, COLS),
            wide(RIM + HALF_ROWS, COLS),
            vmem(2, 2, GROUP, HALF_ROWS, HEAD),
            vmem(2, 2, GROUP, 2, CHUNK, 2 * HEAD),
            vmem(2, 2, GROUP, HEAD, 2 * HEAD),
            wide(2, 2, GROUP, HEAD, 2 * HEAD),
            vmem(inner_count, SLOT, HEAD),
            vmem(inner_count, SLOT, HEAD),
            vmem(inner_count, SLOT, HEAD),
            vmem(inner_count // 2, SLOT, HEAD),
            vmem(SLOT, HEAD),
            vmem(outer_count, SLOT, HEAD),
            vmem(inner_count, HALF, HEAD),
            vmem(inner_count, HALF, HEAD),
            vmem(2, GROUP, ROWS, HEAD),
            wide(2, GROUP, ROWS, HEAD),
            vmem(ROWS, WIDTH),
            dma(9), dma(ROWS // FINISH), dma(2),
            dma(inner_count), dma(inner_count), dma(outer_count), dma(outer_count), dma(inner_count), dma(inner_count),
        ],
        compiler_params=pltpu.CompilerParams(
            collective_id=0, has_side_effects=True, vmem_limit_bytes=63 << 20
        ),
    )(
        byte_states, patch_vectors, patch_starts.reshape(1, PATCHES), beta_codes.T, w_qkv, conv_taps,
        norm_gain.reshape(1, WIDTH), w_out,
    )
    return pl.pallas_call(
        copy_kernel,
        in_specs=[far],
        out_specs=far,
        out_shape=jax.ShapeDtypeStruct((ROWS, WIDTH), BF16),
        scratch_shapes=[vmem(ROWS, WIDTH), dma(PIECES), dma(PIECES)],
        compiler_params=pltpu.CompilerParams(vmem_limit_bytes=63 << 20),
    )(mixed)


def solution(mesh):
    in_specs = (
        P(("outer", "inner"), None),
        P(("outer", "inner"), None),
        P(("outer", "inner")),
        P(("outer", "inner"), None),
        P(),
        P(),
        P(),
        P(),
    )
    out_specs = P(("outer", "inner"), None)
    return jax.shard_map(local, mesh=mesh, in_specs=in_specs, out_specs=out_specs, check_vma=False)
```

```python
import functools

import jax
import jax.numpy as jnp
from jax import lax
from jax.experimental import pallas as pl
from jax.experimental.pallas import tpu as pltpu
from jax.sharding import PartitionSpec as P

HEADS = 8
HEAD = 128
WIDTH = 1024
ROWS = 512
PATCHES = 128
CHUNK = 128
FINISH = 256
PIECES = 4
RIM = 16
HALF_ROWS = ROWS // 2
GROUP = HEADS // 2
COLS = GROUP * HEAD
HALF = HEAD // 2
SLOT = HEAD + HALF
EPS = 1e-6
MESH = pl.DeviceIdType.MESH
F32 = jnp.float32
BF16 = jnp.bfloat16


def mm(a, b):
    return jnp.dot(a.astype(BF16), b.astype(BF16), preferred_element_type=F32)


def mm_nt(a, b):
    return lax.dot_general(
        a.astype(BF16), b.astype(BF16), (((1,), (1,)), ((), ())), preferred_element_type=F32
    )


def silu(v):
    return 0.5 * v * (1.0 + jnp.tanh(0.5 * v))


def grid_of(shape):
    return lax.broadcasted_iota(jnp.int32, shape, 0), lax.broadcasted_iota(jnp.int32, shape, 1)


def level_mask(rows, cols, block):
    same = rows // (2 * block) == cols // (2 * block)
    return same & ((rows // block) % 2 == 1) & ((cols // block) % 2 == 0)


def unit_lower_inverses(lowers):
    rows, cols = grid_of((CHUNK, CHUNK))
    eye = (rows == cols).astype(F32)
    first = level_mask(rows, cols, 1)
    solved = [(eye - jnp.where(first, low, 0.0)) for low in lowers]
    block = 2
    while block < CHUNK:
        mask = level_mask(rows, cols, block)
        halves = [mm(x, jnp.where(mask, low, 0.0)) for x, low in zip(solved, lowers)]
        solved = [x - mm(half, x) for half, x in zip(halves, solved)]
        block *= 2
    return solved


def halves_of(x):
    high = x.astype(BF16)
    return high, (x - high.astype(F32)).astype(BF16)


def gram_of(k):
    high, low = halves_of(k)
    crossed = mm_nt(jnp.concatenate([high, low], axis=1), jnp.concatenate([low, high], axis=1))
    return mm_nt(high, high) + crossed


def role_of(inner):
    z, x = inner // 4, inner % 4
    return (x + z) % 2 * HEADS + z * 2 + x // 2


def inner_of(role):
    z = role % HEADS // 2
    return z * 4 + role % 2 * 2 + (role // HEADS + z) % 2


def joined(earlier, later):
    return earlier + later + mm(earlier, later[:HEAD])


def kernel(
    outer_count, inner_count,
    bytes_hbm, patches_hbm, starts_ref, codes_ref, w_hbm, taps_ref, gain_ref, wout_hbm, out_ref,
    hidden, patches, weights, wout, rim_out, rim_in, betas, ext_k, ext_v, ext_q, unit_keys, solved_ref,
    firsts, pairs, moves, slots, before, tree, total, totals, states, landed, qe, oe,
    mixed, sem_in, sem_out, sem_rim, sem_a, recv_a, sem_b, recv_b, sem_c, recv_c,
):
    outer = lax.axis_index("outer")
    inner = lax.axis_index("inner")
    place = outer * inner_count + inner
    mine = role_of(inner)
    devices = outer_count * inner_count

    loads = [
        pltpu.make_async_copy(bytes_hbm, hidden.at[pl.ds(RIM, ROWS)], sem_in.at[0]),
        pltpu.make_async_copy(patches_hbm, patches, sem_in.at[1]),
    ]
    for at, (part, group) in enumerate([(1, 0), (2, 0), (1, 1), (2, 1), (0, 0), (0, 1)]):
        loads.append(
            pltpu.make_async_copy(
                w_hbm.at[:, pl.ds(part * WIDTH + group * COLS, COLS)], weights.at[part, group], sem_in.at[2 + at]
            )
        )
    loads.append(pltpu.make_async_copy(wout_hbm, wout, sem_in.at[8]))
    for load in loads[:2]:
        load.start()

    barrier = pltpu.get_barrier_semaphore()

    def device_at(index):
        index = lax.rem(index + devices, devices)
        return (index // inner_count, lax.rem(index, inner_count))

    following, preceding = device_at(place + 1), device_at(place - 1)
    for neighbour in (following, preceding):
        pl.semaphore_signal(barrier, inc=1, device_id=neighbour, device_id_type=MESH)
    for step in range(1, inner_count):
        peer = lax.rem(inner + step, inner_count)
        pl.semaphore_signal(barrier, inc=1, device_id=(outer, peer), device_id_type=MESH)
    for step in range(1, outer_count):
        peer = lax.rem(outer + step, outer_count)
        pl.semaphore_signal(barrier, inc=1, device_id=(peer, inner), device_id_type=MESH)

    for load in loads[2:]:
        load.start()

    starts = starts_ref[...]
    rows, cols = grid_of((ROWS, PATCHES))
    positions = rows + place * ROWS
    next_starts = jnp.where(cols == PATCHES - 1, jnp.int32(1 << 30), pltpu.roll(jnp.broadcast_to(starts, (ROWS, PATCHES)), PATCHES - 1, 1))
    chosen = ((positions >= starts) & (positions < next_starts)).astype(BF16)
    open_rows = positions[:, :1] < starts[:, :1]
    for group in range(2):
        turned = codes_ref[group * GROUP : (group + 1) * GROUP, :].astype(F32) * 0.25
        betas[group] = turned.T
    loads[0].wait()
    loads[1].wait()
    tail = hidden[ROWS:, :].astype(F32) + jnp.dot(chosen[ROWS - RIM :], patches[...], preferred_element_type=F32)
    rim_rows, _ = grid_of((RIM, WIDTH))
    rim_out[...] = jnp.where(rim_rows == RIM - 4, patches[PATCHES - 1 :, :].astype(F32), tail).astype(BF16)
    pl.semaphore_wait(barrier, inner_count + outer_count)
    rim_copy = pltpu.make_async_remote_copy(
        src_ref=rim_out, dst_ref=rim_in, send_sem=sem_rim.at[0], recv_sem=sem_rim.at[1],
        device_id=following, device_id_type=MESH,
    )
    rim_copy.start()
    picked = jnp.dot(chosen, patches[...], preferred_element_type=F32)
    hidden[RIM:, :] = (hidden[RIM:, :].astype(F32) + picked).astype(BF16)
    for load in loads[2:6]:
        load.wait()
    rim_copy.wait_recv()
    rim = jnp.where(place > 0, rim_in[...].astype(F32), 0.0)
    hidden[:RIM, :] = rim.astype(BF16)
    can_be_open = pl.ds(RIM, ROWS - PATCHES)
    filled = hidden[can_be_open, :].astype(F32)
    hidden[can_be_open, :] = jnp.where(
        open_rows[: ROWS - PATCHES], filled + rim[RIM - 4 : RIM - 3, :], filled
    ).astype(BF16)

    def activate(part, row_half, group, ext):
        here = hidden[pl.ds(pl.multiple_of(row_half * HALF_ROWS, HALF_ROWS), HALF_ROWS + RIM), :]
        projected = jnp.dot(here, weights[part, group], preferred_element_type=F32)
        ext[...] = projected.astype(BF16).astype(F32)
        lanes = pl.ds(pl.multiple_of(part * WIDTH + group * COLS, COLS), COLS)
        running = taps_ref[0:1, lanes] * ext[RIM - 3 : RIM - 3 + HALF_ROWS, :]
        for tap in range(1, 4):
            running += taps_ref[tap : tap + 1, lanes] * ext[RIM - 3 + tap : RIM - 3 + tap + HALF_ROWS, :]
        return silu(running)

    tile_rows, tile_cols = grid_of((CHUNK, CHUNK))

    def spread(role):
        return pltpu.make_async_remote_copy(
            src_ref=moves.at[role], dst_ref=slots.at[inner], send_sem=sem_a.at[role], recv_sem=recv_a.at[inner],
            device_id=(outer, inner_of(role)), device_id_type=MESH,
        )

    def spread_from(source):
        return pltpu.make_async_remote_copy(
            src_ref=moves.at[role_of(source)], dst_ref=slots.at[source], send_sem=sem_a.at[role_of(source)],
            recv_sem=recv_a.at[source], device_id=(outer, source), device_id_type=MESH,
        )

    def advance(row_half, group):
        keys = activate(1, row_half, group, ext_k.at[row_half])
        values = activate(2, row_half, group, ext_v.at[row_half])
        beta = betas[group, row_half * HALF_ROWS : (row_half + 1) * HALF_ROWS, :]
        items = []
        for head in range(GROUP):
            span = slice(head * HEAD, (head + 1) * HEAD)
            k = keys[:, span]
            k = k * lax.rsqrt(jnp.sum(k * k, axis=1, keepdims=True) + EPS)
            unit_keys[row_half, group, head] = k.astype(BF16)
            for c in range(2):
                part = slice(c * CHUNK, (c + 1) * CHUNK)
                items.append((k[part], values[part, span], beta[part, head : head + 1]))
        lowers = [jnp.where(tile_rows > tile_cols, beta * gram_of(k), 0.0) for k, _, beta in items]
        inverses = unit_lower_inverses(lowers)
        sides = [jnp.concatenate([-beta * k, beta * v], axis=1) for k, v, beta in items]
        rough = [mm(x, side).astype(BF16) for x, side in zip(inverses, sides)]
        missed = [
            side - z.astype(F32) - mm(jnp.concatenate(halves_of(low), axis=1), jnp.concatenate([z, z], axis=0))
            for z, low, side in zip(rough, lowers, sides)
        ]
        solved = [(z.astype(F32) + mm(x, left)).astype(BF16) for z, x, left in zip(rough, inverses, missed)]
        parts = [mm(k.astype(BF16).T, s) for (k, _, _), s in zip(items, solved)]
        for head in range(GROUP):
            first, second = parts[2 * head], parts[2 * head + 1]
            for c in range(2):
                solved_ref[row_half, group, head, c] = solved[2 * head + c]
            firsts[row_half, group, head] = first.astype(BF16)
            pairs[row_half, group, head] = first + second + mm(second[:, :HEAD], first)

    def send(group):
        for head in range(GROUP):
            early, late = pairs[0, group, head], pairs[1, group, head]
            whole = early + late + mm(late[:, :HEAD], early)
            flipped = whole.astype(BF16).T
            move, rest = flipped[:HEAD], flipped[HEAD:]
            for half in range(2):
                role = (group * GROUP + head) * 2 + half
                moves[role, :HEAD, :] = move
                moves[role, HEAD:, :] = rest[half * HALF : (half + 1) * HALF]

        for at in range(2 * GROUP):
            role = group * 2 * GROUP + at

            @pl.when(role != mine)
            def _():
                spread(role).start()

            @pl.when(role == mine)
            def _():
                slots[inner] = moves[role]

    def critical(group, _):
        advance(1, group)
        advance(0, group)
        send(group)
        return 0

    lax.fori_loop(0, 2, critical, 0)

    for load in loads[6:8]:
        load.wait()

    def deferred(step, _):
        row_half, group = step // 2, lax.rem(step, 2)
        queries = activate(0, row_half, group, ext_q)
        late = (row_half == 1).astype(F32)
        for head in range(GROUP):
            span = slice(head * HEAD, (head + 1) * HEAD)
            k = unit_keys[row_half, group, head]
            first = firsts[row_half, group, head]
            state_a = pairs[0, group, head] * late
            state_b = state_a + first.astype(F32) + mm(first[:, :HEAD], state_a)
            for c, state in enumerate((state_a, state_b)):
                part = slice(c * CHUNK, (c + 1) * CHUNK)
                q = queries[part, span]
                score = jnp.where(tile_rows >= tile_cols, mm_nt(q, k[part]), 0.0)
                base = mm(score, solved_ref[row_half, group, head, c])
                reach = base[:, :HEAD] + q
                result = mm(reach, state)
                to = pl.ds(pl.multiple_of(row_half * HALF_ROWS + c * CHUNK, CHUNK), CHUNK)
                qe[group, head, to, :] = (reach + result[:, :HEAD]).astype(BF16)
                oe[group, head, to, :] = base[:, HEAD:] + result[:, HEAD:]
        return 0

    lax.fori_loop(0, 4, deferred, 0)

    for step in range(1, inner_count):
        spread_from(lax.rem(inner + step, inner_count)).wait_recv()
    for at in range(inner_count // 2):
        tree[at] = joined(slots[2 * at].astype(F32), slots[2 * at + 1].astype(F32)).astype(BF16)
    count = inner_count // 4
    while count:
        for at in range(count):
            tree[at] = joined(tree[2 * at].astype(F32), tree[2 * at + 1].astype(F32)).astype(BF16)
        count //= 2
    total[...] = tree[0]

    def outward(peer):
        return pltpu.make_async_remote_copy(
            src_ref=total, dst_ref=totals.at[outer], send_sem=sem_b.at[peer], recv_sem=recv_b.at[outer],
            device_id=(peer, inner), device_id_type=MESH,
        )

    def outward_from(source):
        return pltpu.make_async_remote_copy(
            src_ref=total, dst_ref=totals.at[source], send_sem=sem_b.at[source], recv_sem=recv_b.at[source],
            device_id=(source, inner), device_id_type=MESH,
        )

    for step in range(1, outer_count):
        peer = outer + step

        @pl.when(peer < outer_count)
        def _():
            outward(peer).start()

    running = jnp.zeros((SLOT, HEAD), F32)
    for at in range(inner_count):
        before[at] = running.astype(BF16)
        if at < inner_count - 1:
            running = joined(running, slots[at].astype(F32))

    def descend(source, s):
        outward_from(source).wait_recv()
        return s + mm(s, totals[source, :HEAD, :]) + totals[source, HEAD:, :].astype(F32)

    s = lax.fori_loop(0, outer, descend, jnp.zeros((HALF, HEAD), F32))

    def give(peer):
        return pltpu.make_async_remote_copy(
            src_ref=states.at[peer], dst_ref=landed.at[mine], send_sem=sem_c.at[peer], recv_sem=recv_c.at[mine],
            device_id=(outer, peer), device_id_type=MESH,
        )

    def give_from(source):
        return pltpu.make_async_remote_copy(
            src_ref=states.at[source], dst_ref=landed.at[role_of(source)], send_sem=sem_c.at[source],
            recv_sem=recv_c.at[role_of(source)], device_id=(outer, source), device_id_type=MESH,
        )

    for step in range(1, inner_count + 1):
        peer = lax.rem(inner + step, inner_count)
        at_start = (s + mm(s, before[peer, :HEAD, :]) + before[peer, HEAD:, :].astype(F32)).astype(BF16)
        if step == inner_count:
            landed[mine] = at_start
        else:
            states[peer] = at_start
            give(peer).start()
    loads[8].wait()
    for step in range(1, inner_count):
        give_from(lax.rem(inner + step, inner_count)).wait_recv()

    written = []
    for tile in range(ROWS // FINISH):
        at = slice(tile * FINISH, (tile + 1) * FINISH)
        parts = []
        for head in range(HEADS):
            state = jnp.concatenate([landed[2 * head], landed[2 * head + 1]], axis=0)
            group, inside = head // GROUP, head % GROUP
            result = oe[group, inside, at, :] + mm_nt(qe[group, inside, at, :], state)
            mean = jnp.sum(result * result, axis=1, keepdims=True) * (1.0 / HEAD)
            gain = gain_ref[:, head * HEAD : (head + 1) * HEAD]
            parts.append((result * lax.rsqrt(mean + EPS) * gain).astype(BF16))
        normed = jnp.concatenate(parts, axis=1)
        mixed[at, :] = jnp.dot(normed, wout[...], preferred_element_type=F32).astype(BF16)
        written.append(pltpu.make_async_copy(mixed.at[at], out_ref.at[at], sem_out.at[tile]))
        written[-1].start()

    for copy in written:
        copy.wait()
    rim_copy.wait_send()
    for step in range(1, inner_count):
        peer = lax.rem(inner + step, inner_count)
        spread_from(peer).wait_send()
        give_from(peer).wait_send()
    for step in range(1, outer_count):
        peer = outer + step

        @pl.when(peer < outer_count)
        def _():
            outward(peer).wait_send()


def copy_kernel(from_ref, to_ref, held, sem_from, sem_to):
    pieces = [pl.ds(at * (ROWS // PIECES), ROWS // PIECES) for at in range(PIECES)]
    arriving = [pltpu.make_async_copy(from_ref.at[p], held.at[p], sem_from.at[at]) for at, p in enumerate(pieces)]
    leaving = [pltpu.make_async_copy(held.at[p], to_ref.at[p], sem_to.at[at]) for at, p in enumerate(pieces)]
    for copy in arriving:
        copy.start()
    for first, second in zip(arriving, leaving):
        first.wait()
        second.start()
    for copy in leaving:
        copy.wait()


def local(byte_states, patch_vectors, patch_starts, beta_codes, w_qkv, conv_taps, norm_gain, w_out):
    outer_count, inner_count = lax.axis_size("outer"), lax.axis_size("inner")
    dma = lambda *n: pltpu.SemaphoreType.DMA(n)
    vmem = lambda *shape: pltpu.VMEM(shape, BF16)
    wide = lambda *shape: pltpu.VMEM(shape, F32)
    here, far = pl.BlockSpec(memory_space=pltpu.VMEM), pl.BlockSpec(memory_space=pl.ANY)
    mixed = pl.pallas_call(
        functools.partial(kernel, outer_count, inner_count),
        in_specs=[far, far, here, here, far, here, here, far],
        out_specs=far,
        out_shape=jax.ShapeDtypeStruct((ROWS, WIDTH), BF16),
        scratch_shapes=[
            vmem(RIM + ROWS, WIDTH),
            vmem(PATCHES, WIDTH),
            vmem(3, 2, WIDTH, COLS),
            vmem(WIDTH, WIDTH),
            vmem(RIM, WIDTH),
            vmem(RIM, WIDTH),
            wide(2, ROWS, GROUP),
            wide(2, RIM + HALF_ROWS, COLS),
            wide(2, RIM + HALF_ROWS, COLS),
            wide(RIM + HALF_ROWS, COLS),
            vmem(2, 2, GROUP, HALF_ROWS, HEAD),
            vmem(2, 2, GROUP, 2, CHUNK, 2 * HEAD),
            vmem(2, 2, GROUP, HEAD, 2 * HEAD),
            wide(2, 2, GROUP, HEAD, 2 * HEAD),
            vmem(inner_count, SLOT, HEAD),
            vmem(inner_count, SLOT, HEAD),
            vmem(inner_count, SLOT, HEAD),
            vmem(inner_count // 2, SLOT, HEAD),
            vmem(SLOT, HEAD),
            vmem(outer_count, SLOT, HEAD),
            vmem(inner_count, HALF, HEAD),
            vmem(inner_count, HALF, HEAD),
            vmem(2, GROUP, ROWS, HEAD),
            wide(2, GROUP, ROWS, HEAD),
            vmem(ROWS, WIDTH),
            dma(9), dma(ROWS // FINISH), dma(2),
            dma(inner_count), dma(inner_count), dma(outer_count), dma(outer_count), dma(inner_count), dma(inner_count),
        ],
        compiler_params=pltpu.CompilerParams(
            collective_id=0, has_side_effects=True, vmem_limit_bytes=63 << 20
        ),
    )(
        byte_states, patch_vectors, patch_starts.reshape(1, PATCHES), beta_codes.T, w_qkv, conv_taps,
        norm_gain.reshape(1, WIDTH), w_out,
    )
    return pl.pallas_call(
        copy_kernel,
        in_specs=[far],
        out_specs=far,
        out_shape=jax.ShapeDtypeStruct((ROWS, WIDTH), BF16),
        scratch_shapes=[vmem(ROWS, WIDTH), dma(PIECES), dma(PIECES)],
        compiler_params=pltpu.CompilerParams(vmem_limit_bytes=63 << 20),
    )(mixed)


def solution(mesh):
    in_specs = (
        P(("outer", "inner"), None),
        P(("outer", "inner"), None),
        P(("outer", "inner")),
        P(("outer", "inner"), None),
        P(),
        P(),
        P(),
        P(),
    )
    out_specs = P(("outer", "inner"), None)
    return jax.shard_map(local, mesh=mesh, in_specs=in_specs, out_specs=out_specs, check_vma=False)
```

```python
import functools

import jax
import jax.numpy as jnp
from jax import lax
from jax.experimental import pallas as pl
from jax.experimental.pallas import tpu as pltpu
from jax.sharding import PartitionSpec as P

HEADS = 8
HEAD = 128
WIDTH = 1024
ROWS = 512
PATCHES = 128
CHUNK = 128
FINISH = 256
PIECES = 4
RIM = 16
HALF_ROWS = ROWS // 2
GROUP = HEADS // 2
COLS = GROUP * HEAD
HALF = HEAD // 2
SLOT = HEAD + HALF
EPS = 1e-6
MESH = pl.DeviceIdType.MESH
F32 = jnp.float32
BF16 = jnp.bfloat16


def mm(a, b):
    return jnp.dot(a.astype(BF16), b.astype(BF16), preferred_element_type=F32)


def mm_nt(a, b):
    return lax.dot_general(
        a.astype(BF16), b.astype(BF16), (((1,), (1,)), ((), ())), preferred_element_type=F32
    )


def silu(v):
    return 0.5 * v * (1.0 + jnp.tanh(0.5 * v))


def grid_of(shape):
    return lax.broadcasted_iota(jnp.int32, shape, 0), lax.broadcasted_iota(jnp.int32, shape, 1)


def level_mask(rows, cols, block):
    same = rows // (2 * block) == cols // (2 * block)
    return same & ((rows // block) % 2 == 1) & ((cols // block) % 2 == 0)


def unit_lower_inverses(lowers):
    rows, cols = grid_of((CHUNK, CHUNK))
    eye = (rows == cols).astype(F32)
    first = level_mask(rows, cols, 1)
    solved = [(eye - jnp.where(first, low, 0.0)) for low in lowers]
    for block, growth in ((2, 2), (4, 4), (16, 4), (64, 2)):
        size = block * growth
        mask = (rows // size == cols // size) & (rows // block > cols // block)
        steps = [mm(x, jnp.where(mask, low, 0.0)) for x, low in zip(solved, lowers)]
        if growth == 2:
            solved = [x - mm(step, x) for step, x in zip(steps, solved)]
        else:
            both = [mm(step, jnp.concatenate([step, x], axis=1)) for step, x in zip(steps, solved)]
            once = [x - pair[:, CHUNK:] for x, pair in zip(solved, both)]
            solved = [part + mm(pair[:, :CHUNK], part) for part, pair in zip(once, both)]
    return solved


def halves_of(x):
    high = x.astype(BF16)
    return high, (x - high.astype(F32)).astype(BF16)


def gram_of(k):
    high, low = halves_of(k)
    crossed = mm_nt(jnp.concatenate([high, low], axis=1), jnp.concatenate([low, high], axis=1))
    return mm_nt(high, high) + crossed


def role_of(inner):
    z, x = inner // 4, inner % 4
    return (x + z) % 2 * HEADS + z * 2 + x // 2


def inner_of(role):
    z = role % HEADS // 2
    return z * 4 + role % 2 * 2 + (role // HEADS + z) % 2


def joined(earlier, later):
    return earlier + later + mm(earlier, later[:HEAD])


def kernel(
    outer_count, inner_count,
    bytes_hbm, patches_hbm, starts_ref, codes_ref, w_hbm, taps_ref, gain_ref, wout_hbm, out_ref,
    hidden, patches, weights, wout, rim_out, rim_in, betas, ext_k, ext_v, ext_q, unit_keys, solved_ref,
    firsts, pairs, moves, slots, before, tree, total, totals, states, landed, qe, oe,
    mixed, sem_in, sem_out, sem_rim, sem_a, recv_a, sem_b, recv_b, sem_c, recv_c,
):
    outer = lax.axis_index("outer")
    inner = lax.axis_index("inner")
    place = outer * inner_count + inner
    mine = role_of(inner)
    devices = outer_count * inner_count

    loads = [
        pltpu.make_async_copy(bytes_hbm, hidden.at[pl.ds(RIM, ROWS)], sem_in.at[0]),
        pltpu.make_async_copy(patches_hbm, patches, sem_in.at[1]),
    ]
    for at, (part, group) in enumerate([(1, 0), (2, 0), (1, 1), (2, 1), (0, 0), (0, 1)]):
        loads.append(
            pltpu.make_async_copy(
                w_hbm.at[:, pl.ds(part * WIDTH + group * COLS, COLS)], weights.at[part, group], sem_in.at[2 + at]
            )
        )
    loads.append(pltpu.make_async_copy(wout_hbm, wout, sem_in.at[8]))
    for load in loads[:2]:
        load.start()

    barrier = pltpu.get_barrier_semaphore()

    def device_at(index):
        index = lax.rem(index + devices, devices)
        return (index // inner_count, lax.rem(index, inner_count))

    following, preceding = device_at(place + 1), device_at(place - 1)
    for neighbour in (following, preceding):
        pl.semaphore_signal(barrier, inc=1, device_id=neighbour, device_id_type=MESH)
    for step in range(1, inner_count):
        peer = lax.rem(inner + step, inner_count)
        pl.semaphore_signal(barrier, inc=1, device_id=(outer, peer), device_id_type=MESH)
    for step in range(1, outer_count):
        peer = lax.rem(outer + step, outer_count)
        pl.semaphore_signal(barrier, inc=1, device_id=(peer, inner), device_id_type=MESH)

    for load in loads[2:]:
        load.start()

    starts = starts_ref[...]
    rows, cols = grid_of((ROWS, PATCHES))
    positions = rows + place * ROWS
    next_starts = jnp.where(cols == PATCHES - 1, jnp.int32(1 << 30), pltpu.roll(jnp.broadcast_to(starts, (ROWS, PATCHES)), PATCHES - 1, 1))
    chosen = ((positions >= starts) & (positions < next_starts)).astype(BF16)
    open_rows = positions[:, :1] < starts[:, :1]
    for group in range(2):
        turned = codes_ref[group * GROUP : (group + 1) * GROUP, :].astype(F32) * 0.25
        betas[group] = turned.T
    loads[0].wait()
    loads[1].wait()
    tail = hidden[ROWS:, :].astype(F32) + jnp.dot(chosen[ROWS - RIM :], patches[...], preferred_element_type=F32)
    rim_rows, _ = grid_of((RIM, WIDTH))
    rim_out[...] = jnp.where(rim_rows == RIM - 4, patches[PATCHES - 1 :, :].astype(F32), tail).astype(BF16)
    pl.semaphore_wait(barrier, inner_count + outer_count)
    rim_copy = pltpu.make_async_remote_copy(
        src_ref=rim_out, dst_ref=rim_in, send_sem=sem_rim.at[0], recv_sem=sem_rim.at[1],
        device_id=following, device_id_type=MESH,
    )
    rim_copy.start()
    picked = jnp.dot(chosen, patches[...], preferred_element_type=F32)
    hidden[RIM:, :] = (hidden[RIM:, :].astype(F32) + picked).astype(BF16)
    for load in loads[2:6]:
        load.wait()
    rim_copy.wait_recv()
    rim = jnp.where(place > 0, rim_in[...].astype(F32), 0.0)
    hidden[:RIM, :] = rim.astype(BF16)
    can_be_open = pl.ds(RIM, ROWS - PATCHES)
    filled = hidden[can_be_open, :].astype(F32)
    hidden[can_be_open, :] = jnp.where(
        open_rows[: ROWS - PATCHES], filled + rim[RIM - 4 : RIM - 3, :], filled
    ).astype(BF16)

    def activate(part, row_half, group, ext):
        here = hidden[pl.ds(pl.multiple_of(row_half * HALF_ROWS, HALF_ROWS), HALF_ROWS + RIM), :]
        projected = jnp.dot(here, weights[part, group], preferred_element_type=F32)
        ext[...] = projected.astype(BF16).astype(F32)
        lanes = pl.ds(pl.multiple_of(part * WIDTH + group * COLS, COLS), COLS)
        running = taps_ref[0:1, lanes] * ext[RIM - 3 : RIM - 3 + HALF_ROWS, :]
        for tap in range(1, 4):
            running += taps_ref[tap : tap + 1, lanes] * ext[RIM - 3 + tap : RIM - 3 + tap + HALF_ROWS, :]
        return silu(running)

    tile_rows, tile_cols = grid_of((CHUNK, CHUNK))

    def spread(role):
        return pltpu.make_async_remote_copy(
            src_ref=moves.at[role], dst_ref=slots.at[inner], send_sem=sem_a.at[role], recv_sem=recv_a.at[inner],
            device_id=(outer, inner_of(role)), device_id_type=MESH,
        )

    def spread_from(source):
        return pltpu.make_async_remote_copy(
            src_ref=moves.at[role_of(source)], dst_ref=slots.at[source], send_sem=sem_a.at[role_of(source)],
            recv_sem=recv_a.at[source], device_id=(outer, source), device_id_type=MESH,
        )

    def advance(row_half, group):
        keys = activate(1, row_half, group, ext_k.at[row_half])
        values = activate(2, row_half, group, ext_v.at[row_half])
        beta = betas[group, row_half * HALF_ROWS : (row_half + 1) * HALF_ROWS, :]
        items = []
        for head in range(GROUP):
            span = slice(head * HEAD, (head + 1) * HEAD)
            k = keys[:, span]
            k = k * lax.rsqrt(jnp.sum(k * k, axis=1, keepdims=True) + EPS)
            unit_keys[row_half, group, head] = k.astype(BF16)
            for c in range(2):
                part = slice(c * CHUNK, (c + 1) * CHUNK)
                items.append((k[part], values[part, span], beta[part, head : head + 1]))
        lowers = [jnp.where(tile_rows > tile_cols, beta * gram_of(k), 0.0) for k, _, beta in items]
        inverses = unit_lower_inverses(lowers)
        sides = [jnp.concatenate([-beta * k, beta * v], axis=1) for k, v, beta in items]
        rough = [mm(x, side).astype(BF16) for x, side in zip(inverses, sides)]
        missed = [
            side - z.astype(F32) - mm(jnp.concatenate(halves_of(low), axis=1), jnp.concatenate([z, z], axis=0))
            for z, low, side in zip(rough, lowers, sides)
        ]
        solved = [(z.astype(F32) + mm(x, left)).astype(BF16) for z, x, left in zip(rough, inverses, missed)]
        parts = [mm(k.astype(BF16).T, s) for (k, _, _), s in zip(items, solved)]
        for head in range(GROUP):
            first, second = parts[2 * head], parts[2 * head + 1]
            for c in range(2):
                solved_ref[row_half, group, head, c] = solved[2 * head + c]
            firsts[row_half, group, head] = first.astype(BF16)
            pairs[row_half, group, head] = first + second + mm(second[:, :HEAD], first)

    def send(group):
        for head in range(GROUP):
            early, late = pairs[0, group, head], pairs[1, group, head]
            whole = early + late + mm(late[:, :HEAD], early)
            flipped = whole.astype(BF16).T
            move, rest = flipped[:HEAD], flipped[HEAD:]
            for half in range(2):
                role = (group * GROUP + head) * 2 + half
                moves[role, :HEAD, :] = move
                moves[role, HEAD:, :] = rest[half * HALF : (half + 1) * HALF]

        for at in range(2 * GROUP):
            role = group * 2 * GROUP + at

            @pl.when(role != mine)
            def _():
                spread(role).start()

            @pl.when(role == mine)
            def _():
                slots[inner] = moves[role]

    def critical(group, _):
        advance(1, group)
        advance(0, group)
        send(group)
        return 0

    lax.fori_loop(0, 2, critical, 0)

    for load in loads[6:8]:
        load.wait()

    def deferred(step, _):
        row_half, group = step // 2, lax.rem(step, 2)
        queries = activate(0, row_half, group, ext_q)
        late = (row_half == 1).astype(F32)
        for head in range(GROUP):
            span = slice(head * HEAD, (head + 1) * HEAD)
            k = unit_keys[row_half, group, head]
            first = firsts[row_half, group, head]
            state_a = pairs[0, group, head] * late
            state_b = state_a + first.astype(F32) + mm(first[:, :HEAD], state_a)
            for c, state in enumerate((state_a, state_b)):
                part = slice(c * CHUNK, (c + 1) * CHUNK)
                q = queries[part, span]
                score = jnp.where(tile_rows >= tile_cols, mm_nt(q, k[part]), 0.0)
                base = mm(score, solved_ref[row_half, group, head, c])
                reach = base[:, :HEAD] + q
                result = mm(reach, state)
                to = pl.ds(pl.multiple_of(row_half * HALF_ROWS + c * CHUNK, CHUNK), CHUNK)
                qe[group, head, to, :] = (reach + result[:, :HEAD]).astype(BF16)
                oe[group, head, to, :] = base[:, HEAD:] + result[:, HEAD:]
        return 0

    lax.fori_loop(0, 4, deferred, 0)

    for step in range(1, inner_count):
        spread_from(lax.rem(inner + step, inner_count)).wait_recv()
    for at in range(inner_count // 2):
        tree[at] = joined(slots[2 * at].astype(F32), slots[2 * at + 1].astype(F32)).astype(BF16)
    count = inner_count // 4
    while count:
        for at in range(count):
            tree[at] = joined(tree[2 * at].astype(F32), tree[2 * at + 1].astype(F32)).astype(BF16)
        count //= 2
    total[...] = tree[0]

    def outward(peer):
        return pltpu.make_async_remote_copy(
            src_ref=total, dst_ref=totals.at[outer], send_sem=sem_b.at[peer], recv_sem=recv_b.at[outer],
            device_id=(peer, inner), device_id_type=MESH,
        )

    def outward_from(source):
        return pltpu.make_async_remote_copy(
            src_ref=total, dst_ref=totals.at[source], send_sem=sem_b.at[source], recv_sem=recv_b.at[source],
            device_id=(source, inner), device_id_type=MESH,
        )

    for step in range(1, outer_count):
        peer = outer + step

        @pl.when(peer < outer_count)
        def _():
            outward(peer).start()

    running = jnp.zeros((SLOT, HEAD), F32)
    for at in range(inner_count):
        before[at] = running.astype(BF16)
        if at < inner_count - 1:
            running = joined(running, slots[at].astype(F32))

    def descend(source, s):
        outward_from(source).wait_recv()
        return s + mm(s, totals[source, :HEAD, :]) + totals[source, HEAD:, :].astype(F32)

    s = lax.fori_loop(0, outer, descend, jnp.zeros((HALF, HEAD), F32))

    def give(peer):
        return pltpu.make_async_remote_copy(
            src_ref=states.at[peer], dst_ref=landed.at[mine], send_sem=sem_c.at[peer], recv_sem=recv_c.at[mine],
            device_id=(outer, peer), device_id_type=MESH,
        )

    def give_from(source):
        return pltpu.make_async_remote_copy(
            src_ref=states.at[source], dst_ref=landed.at[role_of(source)], send_sem=sem_c.at[source],
            recv_sem=recv_c.at[role_of(source)], device_id=(outer, source), device_id_type=MESH,
        )

    for step in range(1, inner_count + 1):
        peer = lax.rem(inner + step, inner_count)
        at_start = (s + mm(s, before[peer, :HEAD, :]) + before[peer, HEAD:, :].astype(F32)).astype(BF16)
        if step == inner_count:
            landed[mine] = at_start
        else:
            states[peer] = at_start
            give(peer).start()
    loads[8].wait()
    for step in range(1, inner_count):
        give_from(lax.rem(inner + step, inner_count)).wait_recv()

    written = []
    for tile in range(ROWS // FINISH):
        at = slice(tile * FINISH, (tile + 1) * FINISH)
        parts = []
        for head in range(HEADS):
            state = jnp.concatenate([landed[2 * head], landed[2 * head + 1]], axis=0)
            group, inside = head // GROUP, head % GROUP
            result = oe[group, inside, at, :] + mm_nt(qe[group, inside, at, :], state)
            mean = jnp.sum(result * result, axis=1, keepdims=True) * (1.0 / HEAD)
            gain = gain_ref[:, head * HEAD : (head + 1) * HEAD]
            parts.append((result * lax.rsqrt(mean + EPS) * gain).astype(BF16))
        normed = jnp.concatenate(parts, axis=1)
        mixed[at, :] = jnp.dot(normed, wout[...], preferred_element_type=F32).astype(BF16)
        written.append(pltpu.make_async_copy(mixed.at[at], out_ref.at[at], sem_out.at[tile]))
        written[-1].start()

    for copy in written:
        copy.wait()
    rim_copy.wait_send()
    for step in range(1, inner_count):
        peer = lax.rem(inner + step, inner_count)
        spread_from(peer).wait_send()
        give_from(peer).wait_send()
    for step in range(1, outer_count):
        peer = outer + step

        @pl.when(peer < outer_count)
        def _():
            outward(peer).wait_send()


def copy_kernel(from_ref, to_ref, held, sem_from, sem_to):
    pieces = [pl.ds(at * (ROWS // PIECES), ROWS // PIECES) for at in range(PIECES)]
    arriving = [pltpu.make_async_copy(from_ref.at[p], held.at[p], sem_from.at[at]) for at, p in enumerate(pieces)]
    leaving = [pltpu.make_async_copy(held.at[p], to_ref.at[p], sem_to.at[at]) for at, p in enumerate(pieces)]
    for copy in arriving:
        copy.start()
    for first, second in zip(arriving, leaving):
        first.wait()
        second.start()
    for copy in leaving:
        copy.wait()


def local(byte_states, patch_vectors, patch_starts, beta_codes, w_qkv, conv_taps, norm_gain, w_out):
    outer_count, inner_count = lax.axis_size("outer"), lax.axis_size("inner")
    dma = lambda *n: pltpu.SemaphoreType.DMA(n)
    vmem = lambda *shape: pltpu.VMEM(shape, BF16)
    wide = lambda *shape: pltpu.VMEM(shape, F32)
    here, far = pl.BlockSpec(memory_space=pltpu.VMEM), pl.BlockSpec(memory_space=pl.ANY)
    mixed = pl.pallas_call(
        functools.partial(kernel, outer_count, inner_count),
        in_specs=[far, far, here, here, far, here, here, far],
        out_specs=far,
        out_shape=jax.ShapeDtypeStruct((ROWS, WIDTH), BF16),
        scratch_shapes=[
            vmem(RIM + ROWS, WIDTH),
            vmem(PATCHES, WIDTH),
            vmem(3, 2, WIDTH, COLS),
            vmem(WIDTH, WIDTH),
            vmem(RIM, WIDTH),
            vmem(RIM, WIDTH),
            wide(2, ROWS, GROUP),
            wide(2, RIM + HALF_ROWS, COLS),
            wide(2, RIM + HALF_ROWS, COLS),
            wide(RIM + HALF_ROWS, COLS),
            vmem(2, 2, GROUP, HALF_ROWS, HEAD),
            vmem(2, 2, GROUP, 2, CHUNK, 2 * HEAD),
            vmem(2, 2, GROUP, HEAD, 2 * HEAD),
            wide(2, 2, GROUP, HEAD, 2 * HEAD),
            vmem(inner_count, SLOT, HEAD),
            vmem(inner_count, SLOT, HEAD),
            vmem(inner_count, SLOT, HEAD),
            vmem(inner_count // 2, SLOT, HEAD),
            vmem(SLOT, HEAD),
            vmem(outer_count, SLOT, HEAD),
            vmem(inner_count, HALF, HEAD),
            vmem(inner_count, HALF, HEAD),
            vmem(2, GROUP, ROWS, HEAD),
            wide(2, GROUP, ROWS, HEAD),
            vmem(ROWS, WIDTH),
            dma(9), dma(ROWS // FINISH), dma(2),
            dma(inner_count), dma(inner_count), dma(outer_count), dma(outer_count), dma(inner_count), dma(inner_count),
        ],
        compiler_params=pltpu.CompilerParams(
            collective_id=0, has_side_effects=True, vmem_limit_bytes=63 << 20
        ),
    )(
        byte_states, patch_vectors, patch_starts.reshape(1, PATCHES), beta_codes.T, w_qkv, conv_taps,
        norm_gain.reshape(1, WIDTH), w_out,
    )
    return pl.pallas_call(
        copy_kernel,
        in_specs=[far],
        out_specs=far,
        out_shape=jax.ShapeDtypeStruct((ROWS, WIDTH), BF16),
        scratch_shapes=[vmem(ROWS, WIDTH), dma(PIECES), dma(PIECES)],
        compiler_params=pltpu.CompilerParams(vmem_limit_bytes=63 << 20),
    )(mixed)


def solution(mesh):
    in_specs = (
        P(("outer", "inner"), None),
        P(("outer", "inner"), None),
        P(("outer", "inner")),
        P(("outer", "inner"), None),
        P(),
        P(),
        P(),
        P(),
    )
    out_specs = P(("outer", "inner"), None)
    return jax.shard_map(local, mesh=mesh, in_specs=in_specs, out_specs=out_specs, check_vma=False)
```
